512 devices in a mesh: seq: 64 (over z, x), head: 8 (over y, core).
Axes of the slice: x: 4, y: 4, z: 16, core: 2. Of those that a mesh axis runs over, the one named last changes fastest.
Arguments:
- queries: bfloat16 [8192, 4096], P('seq', 'head'), may hold values from -110 to 110
- keys: bfloat16 [8192, 1024], P('seq', 'head'), may hold values from -5 to 5
- values: bfloat16 [8192, 1024], P('seq', 'head'), may hold values from -24 to 24
- cache_keys: bfloat16 [8192, 1024], P('seq', 'head'), may hold values from -5 to 5
- cache_values: bfloat16 [8192, 1024], P('seq', 'head'), may hold values from -24 to 24
- spans: int32 [32], P('head'), may hold values from 128 to 16384, as said below
- out_weight: bfloat16 [4096, 4096], P('head'), may hold values from -0.09375 to 0.09375
Outputs:
- mixed_t: bfloat16 [4096, 8192], P('head', 'seq')
The draws below stay inside these ranges and needn't reach their ends.
Inputs may be any that keep to these rules, and one draw needn't show every extreme that they name: In every group of 4 consecutive heads exactly 2 spans exceed 4 * 128; those lie between (16384) // 2 and 16384, the others between 128 and 512. All four ends are reached.
All inputs are finite; a program needn't handle non-finite values.
Results may differ from the reference program's by a relative error of at most 0.019.
Values may be sent and summed in bfloat16 or wider, within the bound.
No kernel may reach another device: no remote copies, remote signals or barrier semaphores. Data moves between devices by JAX's collectives and lax.ppermute only.
A program may use at most 128 MiB of HBM per device.

```python
import math
import jax
import jax.numpy as jnp
from jax import lax

D = 4096
HD = 128
GROUP = 4
REACH = 4
TOK_DEV = 128
KV_HEADS = 8
HEADS = 32
WINDOW = 8192
CACHE = 8192


def shared_draws(key):
    query_key, window_key, cached_key = jax.random.split(key, 3)
    query_noise = jnp.clip(jax.random.normal(query_key, (WINDOW, HEADS * HD), jnp.float32), -5.0, 5.0)
    window_draw = jnp.clip(jax.random.normal(window_key, (WINDOW, KV_HEADS * HD), jnp.float32), -5.0, 5.0)
    cached_draw = jnp.clip(jax.random.normal(cached_key, (CACHE, KV_HEADS * HD), jnp.float32), -5.0, 5.0)
    return (query_noise, window_draw, cached_draw)


def draw_queries(key, part):
    query_noise, window_draw, cached_draw = shared_draws(key)
    key = jax.random.fold_in(key, 3)
    target_key = jax.random.fold_in(key, 0)
    targets = jax.random.randint(target_key, (WINDOW, HEADS), 0, CACHE)
    kv_ids = jnp.arange(HEADS, dtype=jnp.int32) // GROUP
    cached_heads = cached_draw.reshape(CACHE, KV_HEADS, HD)
    needles = cached_heads[targets, kv_ids[None, :]].reshape(WINDOW, HEADS * HD)
    strength = 10.0 / math.sqrt(HD)
    noise = query_noise
    query_draw = noise + strength * needles
    return query_draw.astype(jnp.bfloat16)


def draw_keys(key, part):
    query_noise, window_draw, cached_draw = shared_draws(key)
    return window_draw.astype(jnp.bfloat16)


def draw_cache_keys(key, part):
    query_noise, window_draw, cached_draw = shared_draws(key)
    return cached_draw.astype(jnp.bfloat16)


def draw_spans(key, part):
    key = jax.random.fold_in(key, 11)
    total = CACHE + WINDOW
    perm_key, long_key, short_key = jax.random.split(key, 3)
    orders = jax.vmap(lambda one_key: jax.random.permutation(one_key, GROUP))(jax.random.split(perm_key, KV_HEADS))
    orders = orders.reshape(HEADS).astype(jnp.int32)
    long_flag = orders < GROUP // 2
    long_spans = jax.random.randint(long_key, (HEADS,), total // 2, total + 1)
    short_spans = jax.random.randint(short_key, (HEADS,), TOK_DEV, REACH * TOK_DEV + 1)
    spans = jnp.where(long_flag, long_spans, short_spans).astype(jnp.int32)
    first_group = jnp.arange(HEADS, dtype=jnp.int32) < GROUP
    spans = jnp.where(first_group & (orders == 0), total, spans)
    spans = jnp.where(first_group & (orders == 1), total // 2, spans)
    spans = jnp.where(first_group & (orders == GROUP // 2), TOK_DEV, spans)
    spans = jnp.where(first_group & (orders == GROUP // 2 + 1), REACH * TOK_DEV, spans)
    return spans.astype(jnp.int32)


def steps_of(stream_key, dims, cuts, smallest, high):
    factor_of = 1.0
    for position, blocks in cuts:
        draws = jax.random.uniform(jax.random.fold_in(jax.random.fold_in(stream_key, 6), position), (blocks,), jnp.float32, smallest / len(cuts), high / len(cuts))
        factor_of = factor_of * jnp.repeat(jnp.exp(draws), dims[position] // blocks).reshape((-1,) + (1,) * (len(dims) - 1 - position))
    return factor_of


def bell_draw(key, extent, spread, most, pieces=(), held_as=jnp.bfloat16):
    entries = spread * jax.random.normal(key, extent, jnp.float32)
    if pieces:
        entries = entries * steps_of(key, extent, pieces, -0.22, 0.18)
    return jnp.clip(entries, -most, most).astype(held_as)


def setup_inputs(seed: int = 0) -> dict:
    seeds = jax.random.split(jax.random.key(seed), 8)
    queries = draw_queries(jax.random.fold_in(seeds[7], 71), 0)
    keys = draw_keys(jax.random.fold_in(seeds[7], 71), 0)
    values = bell_draw(seeds[2], (WINDOW, KV_HEADS * HD), 4.0, 24.0, ((0, 64), (1, 8)))
    cache_keys = draw_cache_keys(jax.random.fold_in(seeds[7], 71), 0)
    cache_values = bell_draw(seeds[4], (CACHE, KV_HEADS * HD), 4.0, 24.0, ((0, 64), (1, 8)))
    spans = draw_spans(jax.random.fold_in(seeds[7], 71), 0)
    out_weight = bell_draw(seeds[6], (HEADS * HD, D), (HEADS * HD) ** -0.5, 0.09375, ((0, 8),))
    return {"queries": queries, "keys": keys, "values": values, "cache_keys": cache_keys, "cache_values": cache_values, "spans": spans, "out_weight": out_weight}


def reference(queries, keys, values, cache_keys, cache_values, spans, out_weight):
    total = CACHE + WINDOW
    scale = 1.0 / math.sqrt(HD)
    key_all = jnp.concatenate([cache_keys, keys], axis=0).reshape(total, KV_HEADS, HD).transpose(1, 0, 2)
    value_all = jnp.concatenate([cache_values, values], axis=0).reshape(total, KV_HEADS, HD).transpose(1, 0, 2)
    query_heads = queries.reshape(WINDOW, HEADS, HD).transpose(1, 0, 2)
    block_rows = math.gcd(WINDOW, 1024)
    block_count = WINDOW // block_rows
    key_pos = jnp.arange(total, dtype=jnp.int32)

    def one_head(item):
        query_rows, span, head_number = item
        key_rows = key_all[head_number // GROUP].astype(jnp.float32)
        value_rows = value_all[head_number // GROUP].astype(jnp.float32)
        key_cols = key_rows.T

        def one_block(block_number):
            start = block_number * block_rows
            query_block = lax.dynamic_slice_in_dim(query_rows, start, block_rows, 0).astype(jnp.float32)
            scores = jnp.dot(query_block, key_cols, preferred_element_type=jnp.float32, precision=lax.Precision.HIGHEST) * scale
            query_pos = CACHE + start + jnp.arange(block_rows, dtype=jnp.int32)
            allowed = (key_pos[None, :] <= query_pos[:, None]) & (key_pos[None, :] > (query_pos - span)[:, None])
            masked = jnp.where(allowed, scores, -jnp.inf)
            largest = lax.optimization_barrier(jnp.max(masked, axis=1))
            weights = jnp.where(allowed, jnp.exp(masked - largest[:, None]), 0.0)
            rounded = weights.astype(jnp.bfloat16).astype(jnp.float32)
            summed = jnp.dot(rounded, value_rows, preferred_element_type=jnp.float32, precision=lax.Precision.HIGHEST)
            return summed / lax.optimization_barrier(jnp.sum(weights, axis=1))[:, None]
        blocks = lax.map(one_block, jnp.arange(block_count, dtype=jnp.int32))
        return blocks.reshape(WINDOW, HD)
    heads_out = lax.map(one_head, (query_heads, spans, jnp.arange(HEADS, dtype=jnp.int32)))
    attn = heads_out.transpose(1, 0, 2).reshape(WINDOW, HEADS * HD).astype(jnp.bfloat16)
    product = jnp.dot(attn.astype(jnp.float32), out_weight.astype(jnp.float32), preferred_element_type=jnp.float32, precision=lax.Precision.HIGHEST)
    return product.T.astype(jnp.bfloat16)
```

```python
import functools
import math

import jax
import jax.numpy as jnp
from jax import lax
from jax.experimental import pallas as pl
from jax.experimental.pallas import tpu as pltpu
from jax.sharding import Mesh
from jax.sharding import PartitionSpec as P

HD = 128
GROUP = 4
BLOCKS = 8
RING = 8
STATS = 16
PIECE = GROUP * HD + STATS
MASKED = -1e30
FLOOR = -1e29
FACTOR = math.log2(math.e) / math.sqrt(HD)
TILE = 256


def _scores(keys, rows):
    return lax.dot_general(
        keys, rows, (((1,), (1,)), ((), ())), preferred_element_type=jnp.float32
    )


def _weighted(values, weights):
    return lax.dot_general(
        values, weights, (((0,), (0,)), ((), ())), preferred_element_type=jnp.float32
    )


def _write_stats(stats, block, slot, top, total):
    level = jnp.where(total > 0.0, top * FACTOR + jnp.log2(total), MASKED)
    for i in range(3):
        term = level.astype(jnp.bfloat16).astype(jnp.float32)
        stats[block, pl.ds(slot * 4 + i, 1), :] = term
        level = level - term


def attention_kernel(info, queries, *refs):
    kv, (out, scores, stats) = refs[:-3], refs[-3:]
    blocks = []
    for i in range(RING - 1):
        blocks.append((kv[i], 0, True, i))
        blocks.append((kv[i], 2 * HD, False, i))
    blocks.append((kv[RING - 1], 0, True, RING - 1))
    blocks.append((kv[RING], 0, False, RING - 1))
    window = info[8 + RING]
    base = lax.broadcasted_iota(jnp.int32, (HD, TILE), 1) - lax.broadcasted_iota(
        jnp.int32, (HD, TILE), 0
    )
    stats[...] = jnp.zeros_like(stats)
    per = TILE // HD

    def far(step, _):
        slot = step // (BLOCKS // per)
        first = (step % (BLOCKS // per)) * per
        span = info[slot]
        position = info[4] + first * HD
        rows = queries[pl.ds(first, per), slot].reshape(TILE, HD)
        top = jnp.full((8, TILE), FLOOR, jnp.float32)
        for n, (ref, at, cached, i) in enumerate(blocks):
            found = _scores(ref[at : at + HD, :], rows)
            start = info[8 + i]
            if cached:
                allowed = base < span - position + start
            else:
                allowed = base >= start + window - position
            found = jnp.where(allowed, found, MASKED)
            scores[n * HD : (n + 1) * HD, :] = found
            top = jnp.maximum(top, jnp.max(found.reshape(HD // 8, 8, TILE), axis=0))
        top = jnp.max(top, axis=0, keepdims=True)
        total = jnp.zeros((8, TILE), jnp.float32)
        summed = jnp.zeros((HD, TILE), jnp.float32)
        for n, (ref, at, cached, i) in enumerate(blocks):
            weights = jnp.exp2((scores[n * HD : (n + 1) * HD, :] - top) * FACTOR)
            total = total + jnp.sum(weights.reshape(HD // 8, 8, TILE), axis=0)
            summed = summed + _weighted(
                ref[at + HD : at + 2 * HD, :], weights.astype(jnp.bfloat16)
            )
        total = jnp.sum(total, axis=0, keepdims=True)
        normal = summed * (1.0 / jnp.maximum(total, 1e-30))
        for j in range(per):
            cut = slice(j * HD, (j + 1) * HD)
            out[first + j, pl.ds(pl.multiple_of(slot * HD, HD), HD), :] = normal[:, cut].astype(
                jnp.bfloat16
            )
            _write_stats(stats, first + j, slot, top[:, cut], total[:, cut])
        return 0

    lax.fori_loop(0, 2 * BLOCKS // per, far, 0)

    own = info[6]
    near_base = base[:, :HD]

    def near(step, _):
        slot = 2 + step // BLOCKS
        block = step % BLOCKS
        span = info[slot]
        position = info[4] + block * HD
        rows = queries[block, slot]
        earlier = block < own
        wraps = info[5] == 1
        before = info[8 + 1] + jnp.where(wraps, 0, window)
        start = jnp.where(earlier, before, info[8] + window)
        at = pl.multiple_of(jnp.where(wraps, 0, 2 * HD), HD)
        key_rows = jnp.where(earlier, kv[1][pl.ds(at, HD), :], kv[0][2 * HD : 3 * HD, :])
        value_rows = jnp.where(earlier, kv[1][pl.ds(at + HD, HD), :], kv[0][3 * HD :, :])
        found = _scores(key_rows, rows)
        behind = near_base + (position - start)
        allowed = (behind >= 0) & (behind < span)
        found = jnp.where(allowed, found, MASKED)
        top = jnp.maximum(jnp.max(found, axis=0, keepdims=True), FLOOR)
        weights = jnp.exp2((found - top) * FACTOR)
        total = jnp.sum(weights, axis=0, keepdims=True)
        summed = _weighted(value_rows, weights.astype(jnp.bfloat16))
        normal = summed * (1.0 / jnp.maximum(total, 1e-30))
        out[block, pl.ds(pl.multiple_of(slot * HD, HD), HD), :] = normal.astype(jnp.bfloat16)
        _write_stats(stats, block, slot, top, total)
        return 0

    lax.fori_loop(0, 2 * BLOCKS, near, 0)
    out[:, GROUP * HD :, :] = stats[...].astype(jnp.bfloat16)


def attention(info, queries, kv):
    vmem = pl.BlockSpec(memory_space=pltpu.VMEM)
    return pl.pallas_call(
        attention_kernel,
        out_shape=jax.ShapeDtypeStruct((BLOCKS, PIECE, HD), jnp.bfloat16),
        in_specs=[pl.BlockSpec(memory_space=pltpu.SMEM), vmem] + [vmem] * len(kv),
        out_specs=vmem,
        scratch_shapes=[
            pltpu.VMEM((2 * RING * HD, TILE), jnp.float32),
            pltpu.VMEM((BLOCKS, STATS, HD), jnp.float32),
        ],
        compiler_params=pltpu.CompilerParams(vmem_limit_bytes=32 * 2**20),
        cost_estimate=pl.CostEstimate(
            flops=4 * 2048 * 2048 * 128, bytes_accessed=4 * 2**20, transcendentals=2048 * 2048
        ),
    )(info, queries, *kv)


def per_device(queries, keys, values, cache_keys, cache_values, spans, out_weight):
    rows = queries.shape[0]
    k, e, x = lax.axis_index("k"), lax.axis_index("e"), lax.axis_index("x")
    cache_len = rows * RING * BLOCKS
    far = (spans > 4 * rows).astype(jnp.int32)
    before = jnp.cumsum(far) - far
    rank = jnp.where(far == 1, before, 2 + jnp.arange(GROUP, dtype=jnp.int32) - before)
    slots = jnp.arange(GROUP, dtype=jnp.int32)
    order = jnp.sum(jnp.where(rank[None, :] == slots[:, None], slots[None, :], 0), axis=1)
    slot_spans = jnp.sum(jnp.where(rank[None, :] == slots[:, None], spans[None, :], 0), axis=1)

    heads = jnp.take(queries.reshape(rows, GROUP, HD).transpose(1, 0, 2), order, axis=0)
    sent = jnp.broadcast_to(heads[None], (BLOCKS,) + heads.shape)
    grouped = lax.all_to_all(sent, ("e", "x"), 0, 0, tiled=True)

    own = jnp.concatenate([cache_keys, cache_values, keys, values], axis=0)
    up_route = [(i, (i + 1) % RING) for i in range(RING)]
    down_route = [(i, (i - 1) % RING) for i in range(RING)]
    kv, up, down = [own], own, own
    for _ in range(RING // 2 - 1):
        up = lax.ppermute(up, "k", up_route)
        down = lax.ppermute(down, "k", down_route)
        kv += [up, down]
    kv.append(lax.ppermute(up[: 2 * rows], "k", up_route))
    kv.append(lax.ppermute(down[2 * rows :], "k", down_route))
    distances = [0, -1, 1, -2, 2, -3, 3, 4]
    starts = [(((k + d + RING) % RING * 2 + e) * 4 + x) * rows for d in distances]
    info = jnp.concatenate(
        [
            slot_spans,
            jnp.stack(
                [cache_len + k * (BLOCKS * rows), (k == 0).astype(jnp.int32), e * 4 + x, k * 0]
                + starts
                + [k * 0 + cache_len]
            ).astype(jnp.int32),
        ]
    )
    partial = attention(info, grouped, kv)
    parts = lax.all_to_all(partial, ("e", "x"), 0, 0, tiled=True)

    terms = parts[:, GROUP * HD :].reshape(BLOCKS, GROUP, 4, rows).astype(jnp.float32)
    level = terms[:, :, 0] + terms[:, :, 1] + terms[:, :, 2]
    share = jnp.exp2(level - jnp.max(level, axis=0, keepdims=True))
    share = share / jnp.sum(share, axis=0, keepdims=True)
    found = parts[:, : GROUP * HD].reshape(BLOCKS, GROUP, HD, rows).astype(jnp.float32)
    attn = jnp.sum(found * share[:, :, None, :], axis=0).astype(jnp.bfloat16)
    attn = jnp.take(attn, rank, axis=0).reshape(GROUP * HD, rows)
    product = lax.dot_general(
        out_weight, attn, (((0,), (0,)), ((), ())), preferred_element_type=jnp.float32
    ).astype(jnp.bfloat16)
    shares = lax.all_to_all(
        product.reshape(8, -1, rows), ("y", "c"), 0, 0, tiled=True
    )
    return jnp.sum(shares.astype(jnp.float32), axis=0).astype(jnp.bfloat16)


def solution(mesh):
    fine = Mesh(mesh.devices.reshape(RING, 2, 4, 4, 2), ("k", "e", "x", "y", "c"))
    seq, head = ("k", "e", "x"), ("y", "c")
    placed = (P(seq, head),) * 5 + (P(head), P(head, None))
    return jax.shard_map(
        per_device, mesh=fine, in_specs=placed, out_specs=P(head, seq), check_vma=False
    )
```

```python
import math

import jax
import jax.numpy as jnp
from jax import lax
from jax.experimental import pallas as pl
from jax.experimental.pallas import tpu as pltpu
from jax.sharding import Mesh
from jax.sharding import PartitionSpec as P

HD = 128
GROUP = 4
BLOCKS = 8
RING = 8
STATS = 16
PIECE = GROUP * HD + STATS
MASKED = -1e30
FLOOR = -1e29
FACTOR = math.log2(math.e) / math.sqrt(HD)
TILE = 2 * HD
TILES = 2 * BLOCKS * HD // TILE
CACHE = 2 * RING * BLOCKS // 2 * HD
VMEM = pl.BlockSpec(memory_space=pltpu.VMEM)
SMEM = pl.BlockSpec(memory_space=pltpu.SMEM)
NT = (((1,), (1,)), ((), ()))
NN = (((1,), (0,)), ((), ()))


def dot(a, b, dims):
    return lax.dot_general(a, b, dims, preferred_element_type=jnp.float32)


def head_order(spans):
    far = [(spans[h] > 4 * HD).astype(jnp.int32) for h in range(GROUP)]
    order = [jnp.int32(0)] * GROUP
    ahead = jnp.int32(0)
    for h in range(GROUP):
        rank = jnp.where(far[h] == 1, ahead, 2 + h - ahead)
        ahead = ahead + far[h]
        order = [jnp.where(rank == s, h, order[s]) for s in range(GROUP)]
    return order


def prepare_kernel(spans, queries, keys, values, cache_keys, cache_values, own, sent):
    own[0:HD, :] = cache_keys[...]
    own[HD : 2 * HD, :] = cache_values[...]
    own[2 * HD : 3 * HD, :] = keys[...]
    own[3 * HD :, :] = values[...]
    order = head_order(spans)
    for s in range(GROUP):
        rows = queries[:, pl.ds(pl.multiple_of(order[s] * HD, HD), HD)]
        for j in range(BLOCKS):
            sent[j, s] = rows


def place(info, distance):
    k = lax.rem(info[0] + distance + RING, RING)
    return ((k * 2 + info[1]) * 4 + info[2]) * HD


def offsets():
    token = lax.broadcasted_iota(jnp.int32, (HD, TILE), 1)
    return lax.rem(token, HD), token - lax.broadcasted_iota(jnp.int32, (HD, TILE), 0)


def tile_of(t):
    per = TILE // HD
    return t // (BLOCKS // per), t % (BLOCKS // per) * per


def masked_scores(info, spans, order, offset, key_rows, rows, t, cached, start):
    slot, first = tile_of(t)
    position = CACHE + info[0] * (BLOCKS * HD) + first * HD
    found = dot(key_rows, rows, NT)
    if cached:
        allowed = offset < spans[order[slot]] - position + start
    else:
        allowed = offset >= start + CACHE - position
    return jnp.where(allowed, found, MASKED)


def highest(found):
    return jnp.max(found.reshape(HD // 8, 8, found.shape[1]), axis=0)


def first_kernel(info, spans, queries, *refs):
    kv = refs[: RING - 1]
    sums, tops, near, near_tops, keys, flipped, scores = refs[RING - 1 :]
    order = head_order(spans)
    distances = [0, -1, 1, -2, 2, -3, 3]
    blocks = []
    for i in range(RING - 1):
        for half in range(2):
            n = len(blocks)
            blocks.append((half == 0, place(info, distances[i])))
            keys[n * HD : (n + 1) * HD, :] = kv[i][2 * half * HD : (2 * half + 1) * HD, :]
            flipped[0:HD, n * HD : (n + 1) * HD] = kv[i][
                (2 * half + 1) * HD : (2 * half + 2) * HD, :
            ].T
    width = len(blocks) * HD
    flipped[HD:, :] = jnp.ones((STATS, width), jnp.bfloat16)
    column, offset = offsets()

    def score(t):
        slot, first = tile_of(t)
        rows = queries[first : first + TILE // HD, slot].reshape(TILE, HD)
        top = jnp.full((8, TILE), FLOOR, jnp.float32)
        for n, (cached, start) in enumerate(blocks):
            found = masked_scores(
                info, spans, order, offset, keys[n * HD : (n + 1) * HD, :], rows, t, cached, start
            )
            scores[t % 2, n * HD : (n + 1) * HD, :] = found
            top = jnp.maximum(top, highest(found))
        return jnp.max(top, axis=0, keepdims=True)

    def finish(t, top):
        weights = jnp.concatenate(
            [
                jnp.exp2((scores[t % 2, n * HD : (n + 1) * HD, :] - top) * FACTOR).astype(
                    jnp.bfloat16
                )
                for n in range(len(blocks))
            ],
            axis=0,
        )
        sums[t] = dot(flipped[...], weights, NN)
        tops[t] = jnp.broadcast_to(top, (8, TILE))

    own = info[1] * 4 + info[2]
    wraps = info[0] == 0
    at = jnp.where(wraps, 2 * HD, 3 * HD)
    before_keys = keys[pl.ds(pl.multiple_of(at, HD), HD), :]
    before_values = jnp.where(
        wraps, flipped[:, 2 * HD : 3 * HD], flipped[:, 3 * HD : 4 * HD]
    )
    before_start = place(info, -1) + jnp.where(wraps, 0, CACHE)
    own_start = place(info, 0) + CACHE
    span = jnp.where(
        lax.broadcasted_iota(jnp.int32, (HD, TILE), 1) < HD, spans[order[2]], spans[order[3]]
    )
    near_offset = column - lax.broadcasted_iota(jnp.int32, (HD, TILE), 0)
    for b in range(BLOCKS):
        earlier = b < own
        rows = queries[b, 2:4].reshape(TILE, HD)
        found = dot(jnp.where(earlier, before_keys, keys[HD : 2 * HD, :]), rows, NT)
        position = CACHE + (info[0] * BLOCKS + b) * HD
        behind = near_offset + (position - jnp.where(earlier, before_start, own_start))
        found = jnp.where((behind >= 0) & (behind < span), found, MASKED)
        top = jnp.maximum(jnp.max(found, axis=0, keepdims=True), FLOOR)
        weights = jnp.exp2((found - top) * FACTOR).astype(jnp.bfloat16)
        near[b] = dot(jnp.where(earlier, before_values, flipped[:, HD : 2 * HD]), weights, NN)
        near_tops[b] = jnp.broadcast_to(top, (8, TILE))

    top = score(0)
    for t in range(TILES):
        later = score(t + 1) if t + 1 < TILES else None
        finish(t, top)
        top = later


def write_stats(stats, block, slot, top, total):
    level = jnp.where(total > 0.0, top * FACTOR + jnp.log2(total), MASKED)
    for i in range(3):
        term = level.astype(jnp.bfloat16).astype(jnp.float32)
        stats[block, slot * 4 + i : slot * 4 + i + 1, :] = term
        level = level - term


def second_kernel(info, spans, queries, last, sums, tops, near, near_tops, out, stats):
    order = head_order(spans)
    start = place(info, 4)
    _, offset = offsets()
    ones = jnp.ones((STATS, HD), jnp.bfloat16)
    flipped = jnp.concatenate(
        [
            jnp.concatenate([last[HD : 2 * HD, :].T, ones], axis=0),
            jnp.concatenate([last[3 * HD :, :].T, ones], axis=0),
        ],
        axis=1,
    )
    stats[...] = jnp.zeros_like(stats)

    def emit(block, slot, top, summed):
        total = summed[HD : HD + 1, :]
        normal = summed[:HD, :] * (1.0 / jnp.maximum(total, 1e-30))
        out[block, slot * HD : (slot + 1) * HD, :] = normal.astype(jnp.bfloat16)
        write_stats(stats, block, slot, top, total)

    for b in range(BLOCKS):
        for j in range(2):
            cut = slice(j * HD, (j + 1) * HD)
            emit(b, 2 + j, near_tops[b, 0:1, cut], near[b, :, cut])
    for t in range(TILES):
        slot, first = tile_of(t)
        rows = queries[first : first + TILE // HD, slot].reshape(TILE, HD)
        found = [
            masked_scores(
                info, spans, order, offset, last[2 * half * HD : (2 * half + 1) * HD, :],
                rows, t, half == 0, start,
            )
            for half in range(2)
        ]
        before = tops[t, 0:1, :]
        top = jnp.max(jnp.maximum(highest(found[0]), highest(found[1])), axis=0, keepdims=True)
        top = jnp.maximum(top, before)
        weights = [jnp.exp2((f - top) * FACTOR).astype(jnp.bfloat16) for f in found]
        summed = sums[t] * jnp.exp2((before - top) * FACTOR) + dot(
            flipped, jnp.concatenate(weights, axis=0), NN
        )
        for j in range(TILE // HD):
            cut = slice(j * HD, (j + 1) * HD)
            emit(first + j, slot, top[:, cut], summed[:, cut])
    out[:, GROUP * HD :, :] = stats[...].astype(jnp.bfloat16)


def project_kernel(spans, parts, weight, out, attn):
    order = head_order(spans)
    for s in range(GROUP):
        terms = parts[:, GROUP * HD :, :].astype(jnp.float32)
        level = [
            terms[i, 4 * s : 4 * s + 1] + terms[i, 4 * s + 1 : 4 * s + 2] + terms[i, 4 * s + 2 : 4 * s + 3]
            for i in range(BLOCKS)
        ]
        top = level[0]
        for i in range(1, BLOCKS):
            top = jnp.maximum(top, level[i])
        share = [jnp.exp2(v - top) for v in level]
        total = share[0]
        for i in range(1, BLOCKS):
            total = total + share[i]
        summed = jnp.zeros((HD, HD), jnp.float32)
        for i in range(BLOCKS):
            summed = summed + parts[i, s * HD : (s + 1) * HD, :].astype(jnp.float32) * share[i]
        attn[:, pl.ds(pl.multiple_of(order[s] * HD, HD), HD)] = (
            (summed * (1.0 / total)).T.astype(jnp.bfloat16)
        )
    rows = attn[...]
    width = out.shape[2]
    for f in range(out.shape[0]):
        out[f] = dot(rows, weight[:, f * width : (f + 1) * width], NN).astype(jnp.bfloat16)


def total_kernel(shares, out):
    total = shares[0].astype(jnp.float32)
    for i in range(1, shares.shape[0]):
        total = total + shares[i].astype(jnp.float32)
    out[...] = total.T.astype(jnp.bfloat16)


def call(kernel, outs, specs, scratch=(), vmem=24, flops=0, moved=0, exps=0):
    single = not isinstance(outs, list)
    return pl.pallas_call(
        kernel,
        out_shape=outs,
        in_specs=specs,
        out_specs=VMEM if single else [VMEM] * len(outs),
        scratch_shapes=list(scratch),
        compiler_params=pltpu.CompilerParams(vmem_limit_bytes=vmem * 2**20),
        cost_estimate=pl.CostEstimate(flops=flops, bytes_accessed=moved, transcendentals=exps),
    )


def per_device(queries, keys, values, cache_keys, cache_values, spans, out_weight):
    info = jnp.stack([lax.axis_index("k"), lax.axis_index("e"), lax.axis_index("x")])
    bf16, f32 = jnp.bfloat16, jnp.float32
    own, sent = call(
        prepare_kernel,
        [
            jax.ShapeDtypeStruct((4 * HD, HD), bf16),
            jax.ShapeDtypeStruct((BLOCKS, GROUP, HD, HD), bf16),
        ],
        [SMEM] + [VMEM] * 5,
        moved=2**21,
    )(spans, queries, keys, values, cache_keys, cache_values)
    up_route = [(i, (i + 1) % RING) for i in range(RING)]
    down_route = [(i, (i - 1) % RING) for i in range(RING)]
    kv, up, down = [own], own, own
    for _ in range(RING // 2 - 1):
        up = lax.ppermute(up, "k", up_route)
        down = lax.ppermute(down, "k", down_route)
        kv += [up, down]
    last = lax.ppermute(up, "k", up_route)
    grouped = lax.all_to_all(sent, ("e", "x"), 0, 0, tiled=True)

    near_blocks = 2 * (RING - 1)
    state = call(
        first_kernel,
        [
            jax.ShapeDtypeStruct((TILES, HD + STATS, TILE), f32),
            jax.ShapeDtypeStruct((TILES, 8, TILE), f32),
            jax.ShapeDtypeStruct((BLOCKS, HD + STATS, TILE), f32),
            jax.ShapeDtypeStruct((BLOCKS, 8, TILE), f32),
        ],
        [SMEM, SMEM] + [VMEM] * RING,
        [
            pltpu.VMEM((near_blocks * HD, HD), bf16),
            pltpu.VMEM((HD + STATS, near_blocks * HD), bf16),
            pltpu.VMEM((2, near_blocks * HD, TILE), f32),
        ],
        flops=4 * 2048 * 1792 * 128,
        moved=4 * 2**20,
        exps=2048 * 1792,
    )(info, spans, grouped, *kv)
    partial = call(
        second_kernel,
        jax.ShapeDtypeStruct((BLOCKS, PIECE, HD), bf16),
        [SMEM, SMEM] + [VMEM] * 6,
        [pltpu.VMEM((BLOCKS, STATS, HD), f32)],
        flops=4 * 2048 * 256 * 128,
        moved=4 * 2**20,
        exps=2048 * 256,
    )(info, spans, grouped, last, *state)
    parts = lax.all_to_all(partial, ("e", "x"), 0, 0, tiled=True)
    product = call(
        project_kernel,
        jax.ShapeDtypeStruct((8, HD, out_weight.shape[1] // 8), bf16),
        [SMEM, VMEM, VMEM],
        [pltpu.VMEM((HD, GROUP * HD), bf16)],
        flops=2 * 128 * 512 * 4096,
        moved=5 * 2**20,
    )(spans, parts, out_weight)
    shares = lax.all_to_all(product, ("y", "c"), 0, 0, tiled=True)
    return call(
        total_kernel,
        jax.ShapeDtypeStruct((out_weight.shape[1] // 8, HD), bf16),
        [VMEM],
        moved=2**20,
    )(shares)


def solution(mesh):
    fine = Mesh(mesh.devices.reshape(RING, 2, 4, 4, 2), ("k", "e", "x", "y", "c"))
    seq, head = ("k", "e", "x"), ("y", "c")
    placed = (P(seq, head),) * 5 + (P(head), P(head, None))
    return jax.shard_map(
        per_device, mesh=fine, in_specs=placed, out_specs=P(head, seq), check_vma=False
    )
```

```python
import math

import jax
import jax.numpy as jnp
from jax import lax
from jax.experimental import pallas as pl
from jax.experimental.pallas import tpu as pltpu
from jax.sharding import Mesh
from jax.sharding import PartitionSpec as P

HD = 128
GROUP = 4
FAR = 2
BLOCKS = 8
RING = 8
STATS = 16
PIECE = FAR * HD + STATS
MASKED = -1e30
FLOOR = -1e29
FACTOR = math.log2(math.e) / math.sqrt(HD)
TILE = 2 * HD
TILES = FAR * BLOCKS * HD // TILE
CACHE = 2 * RING * BLOCKS // 2 * HD
VMEM = pl.BlockSpec(memory_space=pltpu.VMEM)
SMEM = pl.BlockSpec(memory_space=pltpu.SMEM)
ANY = pl.BlockSpec(memory_space=pl.ANY)
NT = (((1,), (1,)), ((), ()))
NN = (((1,), (0,)), ((), ()))


def dot(a, b, dims):
    return lax.dot_general(a, b, dims, preferred_element_type=jnp.float32)


def head_order(spans):
    far = [(spans[h] > 4 * HD).astype(jnp.int32) for h in range(GROUP)]
    order = [jnp.int32(0)] * GROUP
    ahead = jnp.int32(0)
    for h in range(GROUP):
        rank = jnp.where(far[h] == 1, ahead, 2 + h - ahead)
        ahead = ahead + far[h]
        order = [jnp.where(rank == s, h, order[s]) for s in range(GROUP)]
    return order


def position():
    return lax.axis_index("k"), lax.axis_index("e"), lax.axis_index("x")


def prepare_kernel(
    spans, queries, keys, values, cache_keys, cache_values, own, sent, handed, near_rows, heads, kinds, sems
):
    sources = [cache_keys, cache_values, keys, values]
    copies = [pltpu.make_async_copy(spans, kinds, sems.at[0])]
    copies.append(pltpu.make_async_copy(queries, heads, sems.at[1]))
    for i in range(4):
        copies.append(
            pltpu.make_async_copy(sources[i], own.at[i * HD : (i + 1) * HD, :], sems.at[2 + i])
        )
    for copy in copies:
        copy.start()
    for copy in copies:
        copy.wait()
    k, e, _ = position()
    ends = (k == RING - 1) & (e == 1)
    handed[...] = jnp.where(ends, own[: 2 * HD, :], own[2 * HD :, :])
    order = head_order(kinds)
    for s in range(GROUP):
        rows = heads[:, pl.ds(pl.multiple_of(order[s] * HD, HD), HD)]
        if s < 2:
            for j in range(BLOCKS):
                sent[j, s] = rows
        else:
            near_rows[(s - 2) * HD : (s - 1) * HD, :] = rows


def place(distance):
    k, e, x = position()
    return ((lax.rem(k + distance + RING, RING) * 2 + e) * 4 + x) * HD


def offsets():
    token = lax.broadcasted_iota(jnp.int32, (HD, TILE), 1)
    return lax.rem(token, HD), token - lax.broadcasted_iota(jnp.int32, (HD, TILE), 0)


def tile_of(t):
    per = TILE // HD
    return t // (BLOCKS // per), t % (BLOCKS // per) * per


def masked_scores(spans, order, offset, key_rows, rows, t, cached, start):
    slot, first = tile_of(t)
    begin = CACHE + lax.axis_index("k") * (BLOCKS * HD) + first * HD
    found = dot(key_rows, rows, NT)
    if cached:
        allowed = offset < spans[order[slot]] - begin + start
    else:
        allowed = offset >= start + CACHE - begin
    return jnp.where(allowed, found, MASKED)


def highest(found):
    return jnp.max(found.reshape(HD // 8, 8, found.shape[1]), axis=0)


def first_kernel(spans, queries, *refs):
    kv = refs[: RING - 1]
    sums, tops, keys, flipped, scores = refs[RING - 1 :]
    order = head_order(spans)
    distances = [0, -1, 1, -2, 2, -3, 3]
    blocks = []
    for i in range(RING - 1):
        for half in range(2):
            n = len(blocks)
            blocks.append((half == 0, place(distances[i])))
            keys[n * HD : (n + 1) * HD, :] = kv[i][2 * half * HD : (2 * half + 1) * HD, :]
            flipped[0:HD, n * HD : (n + 1) * HD] = kv[i][
                (2 * half + 1) * HD : (2 * half + 2) * HD, :
            ].T
    width = len(blocks) * HD
    flipped[HD:, :] = jnp.ones((STATS, width), jnp.bfloat16)
    _, offset = offsets()

    def score(t):
        slot, first = tile_of(t)
        rows = queries[first : first + TILE // HD, slot].reshape(TILE, HD)
        top = jnp.full((8, TILE), FLOOR, jnp.float32)
        for n, (cached, start) in enumerate(blocks):
            found = masked_scores(
                spans, order, offset, keys[n * HD : (n + 1) * HD, :], rows, t, cached, start
            )
            scores[t % 2, n * HD : (n + 1) * HD, :] = found
            top = jnp.maximum(top, highest(found))
        return jnp.max(top, axis=0, keepdims=True)

    def finish(t, top):
        weights = jnp.concatenate(
            [
                jnp.exp2((scores[t % 2, n * HD : (n + 1) * HD, :] - top) * FACTOR).astype(
                    jnp.bfloat16
                )
                for n in range(len(blocks))
            ],
            axis=0,
        )
        sums[t] = dot(flipped[...], weights, NN)
        tops[t] = jnp.broadcast_to(top, (8, TILE))

    top = score(0)
    for t in range(TILES):
        later = score(t + 1) if t + 1 < TILES else None
        finish(t, top)
        top = later


def near_kernel(spans, rows, own, gathered, out, blocks, sems):
    order = head_order(spans)
    _, e, x = position()
    k = lax.axis_index("k")
    copies = []
    for j in range(4):
        at = pl.multiple_of(jnp.where(j < x, 4 * HD, 0), 2 * HD)
        copies.append(
            pltpu.make_async_copy(gathered.at[j, pl.ds(at, 2 * HD), :], blocks.at[j], sems.at[j])
        )
        copies[-1].start()
    for copy in copies:
        copy.wait()
    column, _ = offsets()
    behind = column - lax.broadcasted_iota(jnp.int32, (HD, TILE), 0)
    span = jnp.where(
        lax.broadcasted_iota(jnp.int32, (HD, TILE), 1) < HD, spans[order[2]], spans[order[3]]
    )
    found, values = [], []
    for j in range(5):
        if j < 4:
            distance = jnp.where(j < x, x - j, x - j + 4) * HD
            key_rows, value_rows = blocks[j, :HD, :], blocks[j, HD:, :]
        else:
            distance = 0
            key_rows, value_rows = own[2 * HD : 3 * HD, :], own[3 * HD :, :]
        far = behind + distance
        found.append(
            jnp.where((far >= 0) & (far < span), dot(key_rows, rows[...], NT), MASKED)
        )
        values.append(value_rows)
    top = highest(found[0])
    for j in range(1, 5):
        top = jnp.maximum(top, highest(found[j]))
    top = jnp.max(top, axis=0, keepdims=True)
    weights = jnp.concatenate(
        [jnp.exp2((f - top) * FACTOR).astype(jnp.bfloat16) for f in found], axis=0
    )
    flipped = jnp.concatenate([v.T for v in values], axis=1)
    flipped = jnp.concatenate([flipped, jnp.ones((STATS, 5 * HD), jnp.bfloat16)], axis=0)
    summed = dot(flipped, weights, NN)
    normal = summed[:HD, :] * (1.0 / summed[HD : HD + 1, :])
    for s in range(2):
        out[s] = normal[:, s * HD : (s + 1) * HD].T.astype(jnp.bfloat16)


def write_stats(stats, block, slot, top, total):
    level = jnp.where(total > 0.0, top * FACTOR + jnp.log2(total), MASKED)
    for i in range(3):
        term = level.astype(jnp.bfloat16).astype(jnp.float32)
        stats[block, slot * 4 + i : slot * 4 + i + 1, :] = term
        level = level - term


def second_kernel(spans, queries, last, sums, tops, out, stats):
    order = head_order(spans)
    start = place(4)
    _, offset = offsets()
    ones = jnp.ones((STATS, HD), jnp.bfloat16)
    flipped = jnp.concatenate(
        [
            jnp.concatenate([last[HD : 2 * HD, :].T, ones], axis=0),
            jnp.concatenate([last[3 * HD :, :].T, ones], axis=0),
        ],
        axis=1,
    )
    stats[...] = jnp.zeros_like(stats)
    for t in range(TILES):
        slot, first = tile_of(t)
        rows = queries[first : first + TILE // HD, slot].reshape(TILE, HD)
        found = [
            masked_scores(
                spans, order, offset, last[2 * half * HD : (2 * half + 1) * HD, :],
                rows, t, half == 0, start,
            )
            for half in range(2)
        ]
        before = tops[t, 0:1, :]
        top = jnp.max(jnp.maximum(highest(found[0]), highest(found[1])), axis=0, keepdims=True)
        top = jnp.maximum(top, before)
        weights = [jnp.exp2((f - top) * FACTOR).astype(jnp.bfloat16) for f in found]
        summed = sums[t] * jnp.exp2((before - top) * FACTOR) + dot(
            flipped, jnp.concatenate(weights, axis=0), NN
        )
        total = summed[HD : HD + 1, :]
        normal = summed[:HD, :] * (1.0 / jnp.maximum(total, 1e-30))
        for j in range(TILE // HD):
            cut = slice(j * HD, (j + 1) * HD)
            out[first + j, slot * HD : (slot + 1) * HD, :] = normal[:, cut].astype(jnp.bfloat16)
            write_stats(stats, first + j, slot, top[:, cut], total[:, cut])
    out[:, FAR * HD :, :] = stats[...].astype(jnp.bfloat16)


def project_kernel(spans, parts, near, weight, attn, out):
    order = head_order(spans)
    terms = parts[:, FAR * HD :, :].astype(jnp.float32)
    for s in range(FAR):
        level = [
            terms[i, 4 * s : 4 * s + 1] + terms[i, 4 * s + 1 : 4 * s + 2] + terms[i, 4 * s + 2 : 4 * s + 3]
            for i in range(BLOCKS)
        ]
        top = level[0]
        for i in range(1, BLOCKS):
            top = jnp.maximum(top, level[i])
        share = [jnp.exp2(v - top) for v in level]
        total = share[0]
        for i in range(1, BLOCKS):
            total = total + share[i]
        summed = jnp.zeros((HD, HD), jnp.float32)
        for i in range(BLOCKS):
            summed = summed + parts[i, s * HD : (s + 1) * HD, :].astype(jnp.float32) * share[i]
        attn[:, pl.ds(pl.multiple_of(order[s] * HD, HD), HD)] = (
            (summed * (1.0 / total)).T.astype(jnp.bfloat16)
        )
    for s in range(FAR, GROUP):
        attn[:, pl.ds(pl.multiple_of(order[s] * HD, HD), HD)] = near[s - FAR]
    rows = attn[...]
    other = 1 - lax.axis_index("c")
    width = out.shape[2]
    for f in range(out.shape[0]):
        at = pl.multiple_of((2 * f + other) * width, width)
        out[f] = dot(rows, weight[:, pl.ds(at, width)], NN).astype(jnp.bfloat16)


def add_kernel(attn, weight, received, out):
    rows = attn[...]
    mine = lax.axis_index("c")
    width = out.shape[2]
    for f in range(out.shape[0]):
        at = pl.multiple_of((2 * f + mine) * width, width)
        product = dot(rows, weight[:, pl.ds(at, width)], NN)
        out[f] = (product + received[f].astype(jnp.float32)).astype(jnp.bfloat16)


def total_kernel(shares, out):
    total = shares[0].astype(jnp.float32)
    for i in range(1, shares.shape[0]):
        total = total + shares[i].astype(jnp.float32)
    out[...] = total.T.astype(jnp.bfloat16)


def call(kernel, outs, specs, scratch=(), vmem=24, flops=0, moved=0, exps=0):
    single = not isinstance(outs, list)
    return pl.pallas_call(
        kernel,
        out_shape=outs,
        in_specs=specs,
        out_specs=VMEM if single else [VMEM] * len(outs),
        scratch_shapes=list(scratch),
        compiler_params=pltpu.CompilerParams(vmem_limit_bytes=vmem * 2**20),
        cost_estimate=pl.CostEstimate(flops=flops, bytes_accessed=moved, transcendentals=exps),
    )


def per_device(queries, keys, values, cache_keys, cache_values, spans, out_weight):
    bf16, f32 = jnp.bfloat16, jnp.float32
    own, sent, handed, near_rows = call(
        prepare_kernel,
        [
            jax.ShapeDtypeStruct((4 * HD, HD), bf16),
            jax.ShapeDtypeStruct((BLOCKS, FAR, HD, HD), bf16),
            jax.ShapeDtypeStruct((2 * HD, HD), bf16),
            jax.ShapeDtypeStruct((2 * HD, HD), bf16),
        ],
        [ANY] * 6,
        [
            pltpu.VMEM((HD, GROUP * HD), bf16),
            pltpu.SMEM((GROUP,), jnp.int32),
            pltpu.SemaphoreType.DMA((6,)),
        ],
        moved=2**21,
    )(spans, queries, keys, values, cache_keys, cache_values)
    up_route = [(i, (i + 1) % RING) for i in range(RING)]
    down_route = [(i, (i - 1) % RING) for i in range(RING)]
    grouped = lax.all_to_all(sent, ("e", "x"), 0, 0, tiled=True)
    prior = lax.ppermute(
        handed, ("k", "e"), [(i, (i + 1) % (2 * RING)) for i in range(2 * RING)]
    )
    kv, up, down = [own], own, own
    for _ in range(RING // 2 - 1):
        up = lax.ppermute(up, "k", up_route)
        down = lax.ppermute(down, "k", down_route)
        kv += [up, down]
    last = lax.ppermute(up, "k", up_route)
    gathered = lax.all_gather(jnp.concatenate([prior, own, prior], axis=0), "x", axis=0)
    near = call(
        near_kernel,
        jax.ShapeDtypeStruct((2, HD, HD), bf16),
        [SMEM, VMEM, VMEM, ANY],
        [pltpu.VMEM((4, 2 * HD, HD), bf16), pltpu.SemaphoreType.DMA((4,))],
        flops=4 * 256 * 640 * 128,
        moved=2**19,
        exps=256 * 640,
    )(spans, near_rows, own, gathered)

    far_blocks = 2 * (RING - 1)
    state = call(
        first_kernel,
        [
            jax.ShapeDtypeStruct((TILES, HD + STATS, TILE), f32),
            jax.ShapeDtypeStruct((TILES, 8, TILE), f32),
        ],
        [SMEM] + [VMEM] * RING,
        [
            pltpu.VMEM((far_blocks * HD, HD), bf16),
            pltpu.VMEM((HD + STATS, far_blocks * HD), bf16),
            pltpu.VMEM((2, far_blocks * HD, TILE), f32),
        ],
        flops=4 * 2048 * 1792 * 128,
        moved=4 * 2**20,
        exps=2048 * 1792,
    )(spans, grouped, *kv)
    partial = call(
        second_kernel,
        jax.ShapeDtypeStruct((BLOCKS, PIECE, HD), bf16),
        [SMEM] + [VMEM] * 4,
        [pltpu.VMEM((BLOCKS, STATS, HD), f32)],
        flops=4 * 2048 * 256 * 128,
        moved=4 * 2**20,
        exps=2048 * 256,
    )(spans, grouped, last, *state)
    parts = lax.all_to_all(partial, ("e", "x"), 0, 0, tiled=True)
    width = out_weight.shape[1] // 8
    attn, product = call(
        project_kernel,
        [
            jax.ShapeDtypeStruct((HD, GROUP * HD), bf16),
            jax.ShapeDtypeStruct((4, HD, width), bf16),
        ],
        [SMEM, VMEM, VMEM, VMEM],
        flops=128 * 512 * 4096,
        moved=5 * 2**20,
    )(spans, parts, near, out_weight)
    received = lax.ppermute(product, "c", [(0, 1), (1, 0)])
    halves = call(
        add_kernel,
        jax.ShapeDtypeStruct((4, HD, width), bf16),
        [VMEM] * 3,
        flops=128 * 512 * 4096,
        moved=3 * 2**20,
    )(attn, out_weight, received)
    shares = lax.all_to_all(halves, "y", 0, 0, tiled=True)
    return call(
        total_kernel,
        jax.ShapeDtypeStruct((width, HD), bf16),
        [VMEM],
        moved=2**20,
    )(shares)


def solution(mesh):
    fine = Mesh(mesh.devices.reshape(RING, 2, 4, 4, 2), ("k", "e", "x", "y", "c"))
    seq, head = ("k", "e", "x"), ("y", "c")
    placed = (P(seq, head),) * 5 + (P(head), P(head, None))
    return jax.shard_map(
        per_device, mesh=fine, in_specs=placed, out_specs=P(head, seq), check_vma=False
    )
```

```python
import math

import jax
import jax.numpy as jnp
from jax import lax
from jax.experimental import pallas as pl
from jax.experimental.pallas import tpu as pltpu
from jax.sharding import Mesh
from jax.sharding import PartitionSpec as P

HD = 128
GROUP = 4
FAR = 2
BLOCKS = 8
RING = 8
STATS = 16
PIECE = FAR * HD + STATS
MASKED = -1e30
FLOOR = -1e29
FACTOR = math.log2(math.e) / math.sqrt(HD)
TILE = 2 * HD
TILES = FAR * BLOCKS * HD // TILE
CACHE = 2 * RING * BLOCKS // 2 * HD
VMEM = pl.BlockSpec(memory_space=pltpu.VMEM)
SMEM = pl.BlockSpec(memory_space=pltpu.SMEM)
NT = (((1,), (1,)), ((), ()))
NN = (((1,), (0,)), ((), ()))


def dot(a, b, dims):
    return lax.dot_general(a, b, dims, preferred_element_type=jnp.float32)


def head_order(spans):
    far = [(spans[h] > 4 * HD).astype(jnp.int32) for h in range(GROUP)]
    order = [jnp.int32(0)] * GROUP
    ahead = jnp.int32(0)
    for h in range(GROUP):
        rank = jnp.where(far[h] == 1, ahead, 2 + h - ahead)
        ahead = ahead + far[h]
        order = [jnp.where(rank == s, h, order[s]) for s in range(GROUP)]
    return order


def position():
    return lax.axis_index("k"), lax.axis_index("e"), lax.axis_index("x")


def prepare_kernel(spans, queries, own, before, sent, near_rows):
    order = head_order(spans)
    k, e, x = position()
    me = e * 4 + x
    prior = jnp.where(k == 0, before[: 2 * HD, :], before[2 * HD :, :])
    block = own[2 * HD :, :]
    for s in range(GROUP):
        rows = queries[:, pl.ds(pl.multiple_of(order[s] * HD, HD), HD)]
        if s < FAR:
            for j in range(BLOCKS):
                sent[j, s * HD : (s + 1) * HD, :] = rows
        else:
            near_rows[(s - FAR) * HD : (s - FAR + 1) * HD, :] = rows
    for j in range(BLOCKS):
        sent[j, FAR * HD :, :] = jnp.where(j > me, block, prior)


def place(distance):
    k, e, x = position()
    return ((lax.rem(k + distance + RING, RING) * 2 + e) * 4 + x) * HD


def offsets():
    token = lax.broadcasted_iota(jnp.int32, (HD, TILE), 1)
    return lax.rem(token, HD), token - lax.broadcasted_iota(jnp.int32, (HD, TILE), 0)


def tile_of(t):
    per = TILE // HD
    return t // (BLOCKS // per), t % (BLOCKS // per) * per


def masked_scores(spans, order, offset, key_rows, rows, t, cached, start):
    slot, first = tile_of(t)
    begin = CACHE + lax.axis_index("k") * (BLOCKS * HD) + first * HD
    found = dot(key_rows, rows, NT)
    if cached:
        allowed = offset < spans[order[slot]] - begin + start
    else:
        allowed = offset >= start + CACHE - begin
    return jnp.where(allowed, found, MASKED)


def highest(found):
    return jnp.max(found.reshape(HD // 8, 8, found.shape[1]), axis=0)


def first_kernel(spans, queries, *refs):
    kv = refs[: RING - 1]
    sums, tops, keys, flipped, scores = refs[RING - 1 :]
    order = head_order(spans)
    distances = [0, -1, 1, -2, 2, -3, 3]
    blocks = []
    for i in range(RING - 1):
        for half in range(2):
            n = len(blocks)
            blocks.append((half == 0, place(distances[i])))
            keys[n * HD : (n + 1) * HD, :] = kv[i][2 * half * HD : (2 * half + 1) * HD, :]
            flipped[0:HD, n * HD : (n + 1) * HD] = kv[i][
                (2 * half + 1) * HD : (2 * half + 2) * HD, :
            ].T
    width = len(blocks) * HD
    flipped[HD:, :] = jnp.ones((STATS, width), jnp.bfloat16)
    _, offset = offsets()

    def score(t):
        slot, first = tile_of(t)
        rows = queries[first : first + TILE // HD, slot * HD : (slot + 1) * HD, :].reshape(TILE, HD)
        top = jnp.full((8, TILE), FLOOR, jnp.float32)
        for n, (cached, start) in enumerate(blocks):
            found = masked_scores(
                spans, order, offset, keys[n * HD : (n + 1) * HD, :], rows, t, cached, start
            )
            scores[t % 2, n * HD : (n + 1) * HD, :] = found
            top = jnp.maximum(top, highest(found))
        return jnp.max(top, axis=0, keepdims=True)

    def finish(t, top):
        weights = jnp.concatenate(
            [
                jnp.exp2((scores[t % 2, n * HD : (n + 1) * HD, :] - top) * FACTOR).astype(
                    jnp.bfloat16
                )
                for n in range(len(blocks))
            ],
            axis=0,
        )
        sums[t] = dot(flipped[...], weights, NN)
        tops[t] = jnp.broadcast_to(top, (8, TILE))

    top = score(0)
    for t in range(TILES):
        later = score(t + 1) if t + 1 < TILES else None
        finish(t, top)
        top = later


def near_kernel(spans, rows, own, grouped, out):
    order = head_order(spans)
    _, e, x = position()
    me = e * 4 + x
    column, _ = offsets()
    behind = column - lax.broadcasted_iota(jnp.int32, (HD, TILE), 0)
    span = jnp.where(
        lax.broadcasted_iota(jnp.int32, (HD, TILE), 1) < HD, spans[order[2]], spans[order[3]]
    )
    found, values = [], []
    for j in range(5):
        if j:
            block = grouped[lax.rem(me - j + BLOCKS, BLOCKS), FAR * HD :, :]
        else:
            block = own[2 * HD :, :]
        far = behind + j * HD
        found.append(
            jnp.where((far >= 0) & (far < span), dot(block[:HD, :], rows[...], NT), MASKED)
        )
        values.append(block[HD:, :])
    top = highest(found[0])
    for j in range(1, 5):
        top = jnp.maximum(top, highest(found[j]))
    top = jnp.max(top, axis=0, keepdims=True)
    weights = jnp.concatenate(
        [jnp.exp2((f - top) * FACTOR).astype(jnp.bfloat16) for f in found], axis=0
    )
    flipped = jnp.concatenate([v.T for v in values], axis=1)
    flipped = jnp.concatenate([flipped, jnp.ones((STATS, 5 * HD), jnp.bfloat16)], axis=0)
    summed = dot(flipped, weights, NN)
    normal = summed[:HD, :] * (1.0 / summed[HD : HD + 1, :])
    for s in range(2):
        out[s] = normal[:, s * HD : (s + 1) * HD].T.astype(jnp.bfloat16)


def write_stats(stats, block, slot, top, total):
    level = jnp.where(total > 0.0, top * FACTOR + jnp.log2(total), MASKED)
    for i in range(3):
        term = level.astype(jnp.bfloat16).astype(jnp.float32)
        stats[block, slot * 4 + i : slot * 4 + i + 1, :] = term
        level = level - term


def second_kernel(spans, queries, last, sums, tops, out, stats):
    order = head_order(spans)
    start = place(4)
    _, offset = offsets()
    ones = jnp.ones((STATS, HD), jnp.bfloat16)
    flipped = jnp.concatenate(
        [
            jnp.concatenate([last[HD : 2 * HD, :].T, ones], axis=0),
            jnp.concatenate([last[3 * HD :, :].T, ones], axis=0),
        ],
        axis=1,
    )
    stats[...] = jnp.zeros_like(stats)
    for t in range(TILES):
        slot, first = tile_of(t)
        rows = queries[first : first + TILE // HD, slot * HD : (slot + 1) * HD, :].reshape(TILE, HD)
        found = [
            masked_scores(
                spans, order, offset, last[2 * half * HD : (2 * half + 1) * HD, :],
                rows, t, half == 0, start,
            )
            for half in range(2)
        ]
        before = tops[t, 0:1, :]
        top = jnp.max(jnp.maximum(highest(found[0]), highest(found[1])), axis=0, keepdims=True)
        top = jnp.maximum(top, before)
        weights = [jnp.exp2((f - top) * FACTOR).astype(jnp.bfloat16) for f in found]
        summed = sums[t] * jnp.exp2((before - top) * FACTOR) + dot(
            flipped, jnp.concatenate(weights, axis=0), NN
        )
        total = summed[HD : HD + 1, :]
        normal = summed[:HD, :] * (1.0 / jnp.maximum(total, 1e-30))
        for j in range(TILE // HD):
            cut = slice(j * HD, (j + 1) * HD)
            out[first + j, slot * HD : (slot + 1) * HD, :] = normal[:, cut].astype(jnp.bfloat16)
            write_stats(stats, first + j, slot, top[:, cut], total[:, cut])
    out[:, FAR * HD :, :] = stats[...].astype(jnp.bfloat16)


def project_kernel(spans, parts, near, weight, attn, out):
    order = head_order(spans)
    terms = parts[:, FAR * HD :, :].astype(jnp.float32)
    for s in range(FAR):
        level = [
            terms[i, 4 * s : 4 * s + 1] + terms[i, 4 * s + 1 : 4 * s + 2] + terms[i, 4 * s + 2 : 4 * s + 3]
            for i in range(BLOCKS)
        ]
        top = level[0]
        for i in range(1, BLOCKS):
            top = jnp.maximum(top, level[i])
        share = [jnp.exp2(v - top) for v in level]
        total = share[0]
        for i in range(1, BLOCKS):
            total = total + share[i]
        summed = jnp.zeros((HD, HD), jnp.float32)
        for i in range(BLOCKS):
            summed = summed + parts[i, s * HD : (s + 1) * HD, :].astype(jnp.float32) * share[i]
        attn[:, pl.ds(pl.multiple_of(order[s] * HD, HD), HD)] = (
            (summed * (1.0 / total)).T.astype(jnp.bfloat16)
        )
    for s in range(FAR, GROUP):
        attn[:, pl.ds(pl.multiple_of(order[s] * HD, HD), HD)] = near[s - FAR]
    rows = attn[...]
    other = 1 - lax.axis_index("c")
    width = out.shape[2]
    for f in range(out.shape[0]):
        at = pl.multiple_of((2 * f + other) * width, width)
        out[f] = dot(rows, weight[:, pl.ds(at, width)], NN).astype(jnp.bfloat16)


def add_kernel(attn, weight, received, out):
    rows = attn[...]
    mine = lax.axis_index("c")
    width = out.shape[2]
    for f in range(out.shape[0]):
        at = pl.multiple_of((2 * f + mine) * width, width)
        product = dot(rows, weight[:, pl.ds(at, width)], NN)
        out[f] = (product + received[f].astype(jnp.float32)).astype(jnp.bfloat16)


def total_kernel(shares, out):
    total = shares[0].astype(jnp.float32)
    for i in range(1, shares.shape[0]):
        total = total + shares[i].astype(jnp.float32)
    out[...] = total.T.astype(jnp.bfloat16)


def call(kernel, outs, specs, scratch=(), vmem=12, flops=0, moved=0, exps=0):
    single = not isinstance(outs, list)
    return pl.pallas_call(
        kernel,
        out_shape=outs,
        in_specs=specs,
        out_specs=VMEM if single else [VMEM] * len(outs),
        scratch_shapes=list(scratch),
        compiler_params=pltpu.CompilerParams(vmem_limit_bytes=vmem * 2**20),
        cost_estimate=pl.CostEstimate(flops=flops, bytes_accessed=moved, transcendentals=exps),
    )


def per_device(queries, keys, values, cache_keys, cache_values, spans, out_weight):
    bf16, f32 = jnp.bfloat16, jnp.float32
    own = jnp.concatenate([cache_keys, cache_values, keys, values], axis=0)
    up_route = [(i, (i + 1) % RING) for i in range(RING)]
    down_route = [(i, (i - 1) % RING) for i in range(RING)]
    kv, up, down = [own], own, own
    for _ in range(RING // 2 - 1):
        up = lax.ppermute(up, "k", up_route)
        down = lax.ppermute(down, "k", down_route)
        kv += [up, down]
    last = lax.ppermute(up, "k", up_route)
    sent, near_rows = call(
        prepare_kernel,
        [
            jax.ShapeDtypeStruct((BLOCKS, GROUP * HD, HD), bf16),
            jax.ShapeDtypeStruct((2 * HD, HD), bf16),
        ],
        [SMEM] + [VMEM] * 3,
        moved=2**21,
    )(spans, queries, own, kv[1])
    grouped = lax.all_to_all(sent, ("e", "x"), 0, 0, tiled=True)
    near = call(
        near_kernel,
        jax.ShapeDtypeStruct((2, HD, HD), bf16),
        [SMEM] + [VMEM] * 3,
        flops=4 * 256 * 640 * 128,
        moved=2**19,
        exps=256 * 640,
    )(spans, near_rows, own, grouped)

    far_blocks = 2 * (RING - 1)
    state = call(
        first_kernel,
        [
            jax.ShapeDtypeStruct((TILES, HD + STATS, TILE), f32),
            jax.ShapeDtypeStruct((TILES, 8, TILE), f32),
        ],
        [SMEM] + [VMEM] * RING,
        [
            pltpu.VMEM((far_blocks * HD, HD), bf16),
            pltpu.VMEM((HD + STATS, far_blocks * HD), bf16),
            pltpu.VMEM((2, far_blocks * HD, TILE), f32),
        ],
        flops=4 * 2048 * 1792 * 128,
        moved=4 * 2**20,
        exps=2048 * 1792,
    )(spans, grouped, *kv)
    partial = call(
        second_kernel,
        jax.ShapeDtypeStruct((BLOCKS, PIECE, HD), bf16),
        [SMEM] + [VMEM] * 4,
        [pltpu.VMEM((BLOCKS, STATS, HD), f32)],
        flops=4 * 2048 * 256 * 128,
        moved=4 * 2**20,
        exps=2048 * 256,
    )(spans, grouped, last, *state)
    parts = lax.all_to_all(partial, ("e", "x"), 0, 0, tiled=True)
    width = out_weight.shape[1] // 8
    attn, product = call(
        project_kernel,
        [
            jax.ShapeDtypeStruct((HD, GROUP * HD), bf16),
            jax.ShapeDtypeStruct((4, HD, width), bf16),
        ],
        [SMEM, VMEM, VMEM, VMEM],
        flops=128 * 512 * 4096,
        moved=5 * 2**20,
    )(spans, parts, near, out_weight)
    received = lax.ppermute(product, "c", [(0, 1), (1, 0)])
    halves = call(
        add_kernel,
        jax.ShapeDtypeStruct((4, HD, width), bf16),
        [VMEM] * 3,
        flops=128 * 512 * 4096,
        moved=3 * 2**20,
    )(attn, out_weight, received)
    shares = lax.all_to_all(halves, "y", 0, 0, tiled=True)
    return call(
        total_kernel,
        jax.ShapeDtypeStruct((width, HD), bf16),
        [VMEM],
        moved=2**20,
    )(shares)


def solution(mesh):
    fine = Mesh(mesh.devices.reshape(RING, 2, 4, 4, 2), ("k", "e", "x", "y", "c"))
    seq, head = ("k", "e", "x"), ("y", "c")
    placed = (P(seq, head),) * 5 + (P(head), P(head, None))
    return jax.shard_map(
        per_device, mesh=fine, in_specs=placed, out_specs=P(head, seq), check_vma=False
    )
```

```python
import math

import jax
import jax.numpy as jnp
from jax import lax
from jax.experimental import pallas as pl
from jax.experimental.pallas import tpu as pltpu
from jax.sharding import Mesh
from jax.sharding import PartitionSpec as P

HD = 128
GROUP = 4
FAR = 2
BLOCKS = 8
RING = 8
STATS = 16
PIECE = FAR * HD + STATS
MASKED = -1e30
FLOOR = -1e29
FACTOR = math.log2(math.e) / math.sqrt(HD)
TILE = 2 * HD
TILES = FAR * BLOCKS * HD // TILE
CACHE = 2 * RING * BLOCKS // 2 * HD
VMEM = pl.BlockSpec(memory_space=pltpu.VMEM)
SMEM = pl.BlockSpec(memory_space=pltpu.SMEM)
ANY = pl.BlockSpec(memory_space=pl.ANY)
NT = (((1,), (1,)), ((), ()))
NN = (((1,), (0,)), ((), ()))


def dot(a, b, dims):
    return lax.dot_general(a, b, dims, preferred_element_type=jnp.float32)


def head_order(spans):
    far = [(spans[h] > 4 * HD).astype(jnp.int32) for h in range(GROUP)]
    order = [jnp.int32(0)] * GROUP
    ahead = jnp.int32(0)
    for h in range(GROUP):
        rank = jnp.where(far[h] == 1, ahead, 2 + h - ahead)
        ahead = ahead + far[h]
        order = [jnp.where(rank == s, h, order[s]) for s in range(GROUP)]
    return order


def position():
    return lax.axis_index("k"), lax.axis_index("e"), lax.axis_index("x")


def prepare_kernel(
    spans, queries, keys, values, cache_keys, cache_values, own, sent, near_rows, heads, kinds, sems
):
    copies = [
        pltpu.make_async_copy(spans, kinds, sems.at[0]),
        pltpu.make_async_copy(queries, heads, sems.at[1]),
    ]
    for i, source in enumerate([cache_keys, cache_values, keys, values]):
        copies.append(
            pltpu.make_async_copy(source, own.at[i * HD : (i + 1) * HD, :], sems.at[2 + i])
        )
    for copy in copies:
        copy.start()
    for copy in copies:
        copy.wait()
    order = head_order(kinds)
    for s in range(GROUP):
        rows = heads[:, pl.ds(pl.multiple_of(order[s] * HD, HD), HD)]
        if s < FAR:
            for j in range(BLOCKS):
                sent[j, s * HD : (s + 1) * HD, :] = rows
        else:
            near_rows[(s - FAR) * HD : (s - FAR + 1) * HD, :] = rows


def hand_kernel(own, before, sent, held):
    k, e, x = position()
    me = e * 4 + x
    prior = jnp.where(k == 0, before[: 2 * HD, :], before[2 * HD :, :])
    block = own[2 * HD :, :]
    for j in range(BLOCKS):
        sent[j] = jnp.where(j > me, block, prior)
    held[...] = own[...]


def place(distance):
    k, e, x = position()
    return ((lax.rem(k + distance + RING, RING) * 2 + e) * 4 + x) * HD


def offsets():
    token = lax.broadcasted_iota(jnp.int32, (HD, TILE), 1)
    return lax.rem(token, HD), token - lax.broadcasted_iota(jnp.int32, (HD, TILE), 0)


def tile_of(t):
    per = TILE // HD
    return t // (BLOCKS // per), t % (BLOCKS // per) * per


def masked_scores(spans, order, offset, key_rows, rows, t, cached, start):
    slot, first = tile_of(t)
    begin = CACHE + lax.axis_index("k") * (BLOCKS * HD) + first * HD
    found = dot(key_rows, rows, NT)
    if cached:
        allowed = offset < spans[order[slot]] - begin + start
    else:
        allowed = offset >= start + CACHE - begin
    return jnp.where(allowed, found, MASKED)


def highest(found):
    return jnp.max(found.reshape(HD // 8, 8, found.shape[1]), axis=0)


def first_kernel(spans, queries, *refs):
    kv = refs[: RING - 1]
    sums, tops, keys, flipped, scores = refs[RING - 1 :]
    order = head_order(spans)
    distances = [0, -1, 1, -2, 2, -3, 3]
    blocks = []
    for i in range(RING - 1):
        for half in range(2):
            n = len(blocks)
            blocks.append((half == 0, place(distances[i])))
            keys[n * HD : (n + 1) * HD, :] = kv[i][2 * half * HD : (2 * half + 1) * HD, :]
            flipped[0:HD, n * HD : (n + 1) * HD] = kv[i][
                (2 * half + 1) * HD : (2 * half + 2) * HD, :
            ].T
    width = len(blocks) * HD
    flipped[HD:, :] = jnp.ones((STATS, width), jnp.bfloat16)
    _, offset = offsets()

    def score(t):
        slot, first = tile_of(t)
        rows = queries[first : first + TILE // HD, slot * HD : (slot + 1) * HD, :].reshape(TILE, HD)
        top = jnp.full((8, TILE), FLOOR, jnp.float32)
        for n, (cached, start) in enumerate(blocks):
            found = masked_scores(
                spans, order, offset, keys[n * HD : (n + 1) * HD, :], rows, t, cached, start
            )
            scores[t % 2, n * HD : (n + 1) * HD, :] = found
            top = jnp.maximum(top, highest(found))
        return jnp.max(top, axis=0, keepdims=True)

    def finish(t, top):
        weights = jnp.concatenate(
            [
                jnp.exp2((scores[t % 2, n * HD : (n + 1) * HD, :] - top) * FACTOR).astype(
                    jnp.bfloat16
                )
                for n in range(len(blocks))
            ],
            axis=0,
        )
        sums[t] = dot(flipped[...], weights, NN)
        tops[t] = jnp.broadcast_to(top, (8, TILE))

    top = score(0)
    for t in range(TILES):
        later = score(t + 1) if t + 1 < TILES else None
        finish(t, top)
        top = later


def near_kernel(spans, rows, own, grouped, out):
    order = head_order(spans)
    _, e, x = position()
    me = e * 4 + x
    column, _ = offsets()
    behind = column - lax.broadcasted_iota(jnp.int32, (HD, TILE), 0)
    span = jnp.where(
        lax.broadcasted_iota(jnp.int32, (HD, TILE), 1) < HD, spans[order[2]], spans[order[3]]
    )
    found, values = [], []
    for j in range(5):
        if j:
            block = grouped[lax.rem(me - j + BLOCKS, BLOCKS)]
        else:
            block = own[2 * HD :, :]
        far = behind + j * HD
        found.append(
            jnp.where((far >= 0) & (far < span), dot(block[:HD, :], rows[...], NT), MASKED)
        )
        values.append(block[HD:, :])
    top = highest(found[0])
    for j in range(1, 5):
        top = jnp.maximum(top, highest(found[j]))
    top = jnp.max(top, axis=0, keepdims=True)
    weights = jnp.concatenate(
        [jnp.exp2((f - top) * FACTOR).astype(jnp.bfloat16) for f in found], axis=0
    )
    flipped = jnp.concatenate([v.T for v in values], axis=1)
    flipped = jnp.concatenate([flipped, jnp.ones((STATS, 5 * HD), jnp.bfloat16)], axis=0)
    summed = dot(flipped, weights, NN)
    normal = summed[:HD, :] * (1.0 / summed[HD : HD + 1, :])
    for s in range(2):
        out[s] = normal[:, s * HD : (s + 1) * HD].T.astype(jnp.bfloat16)


def write_stats(stats, block, slot, top, total):
    level = jnp.where(total > 0.0, top * FACTOR + jnp.log2(total), MASKED)
    for i in range(3):
        term = level.astype(jnp.bfloat16).astype(jnp.float32)
        stats[block, slot * 4 + i : slot * 4 + i + 1, :] = term
        level = level - term


def second_kernel(spans, queries, last, sums, tops, out, stats):
    order = head_order(spans)
    start = place(4)
    _, offset = offsets()
    ones = jnp.ones((STATS, HD), jnp.bfloat16)
    flipped = jnp.concatenate(
        [
            jnp.concatenate([last[HD : 2 * HD, :].T, ones], axis=0),
            jnp.concatenate([last[3 * HD :, :].T, ones], axis=0),
        ],
        axis=1,
    )
    stats[...] = jnp.zeros_like(stats)
    for t in range(TILES):
        slot, first = tile_of(t)
        rows = queries[first : first + TILE // HD, slot * HD : (slot + 1) * HD, :].reshape(TILE, HD)
        found = [
            masked_scores(
                spans, order, offset, last[2 * half * HD : (2 * half + 1) * HD, :],
                rows, t, half == 0, start,
            )
            for half in range(2)
        ]
        before = tops[t, 0:1, :]
        top = jnp.max(jnp.maximum(highest(found[0]), highest(found[1])), axis=0, keepdims=True)
        top = jnp.maximum(top, before)
        weights = [jnp.exp2((f - top) * FACTOR).astype(jnp.bfloat16) for f in found]
        summed = sums[t] * jnp.exp2((before - top) * FACTOR) + dot(
            flipped, jnp.concatenate(weights, axis=0), NN
        )
        total = summed[HD : HD + 1, :]
        normal = summed[:HD, :] * (1.0 / jnp.maximum(total, 1e-30))
        for j in range(TILE // HD):
            cut = slice(j * HD, (j + 1) * HD)
            out[first + j, slot * HD : (slot + 1) * HD, :] = normal[:, cut].astype(jnp.bfloat16)
            write_stats(stats, first + j, slot, top[:, cut], total[:, cut])
    out[:, FAR * HD :, :] = stats[...].astype(jnp.bfloat16)


def project_kernel(spans, parts, near, weight, out, kept, attn, columns, sems):
    mine = lax.axis_index("c")
    width = out.shape[2]
    copies = []
    for i in range(2 * out.shape[0]):
        core = mine if i >= out.shape[0] else 1 - mine
        at = pl.multiple_of((2 * (i % out.shape[0]) + core) * width, width)
        copies.append(
            pltpu.make_async_copy(weight.at[:, pl.ds(at, width)], columns.at[i], sems.at[i])
        )
        copies[-1].start()
    order = head_order(spans)
    terms = parts[:, FAR * HD :, :].astype(jnp.float32)
    for s in range(FAR):
        level = [
            terms[i, 4 * s : 4 * s + 1] + terms[i, 4 * s + 1 : 4 * s + 2] + terms[i, 4 * s + 2 : 4 * s + 3]
            for i in range(BLOCKS)
        ]
        top = level[0]
        for i in range(1, BLOCKS):
            top = jnp.maximum(top, level[i])
        share = [jnp.exp2(v - top) for v in level]
        total = share[0]
        for i in range(1, BLOCKS):
            total = total + share[i]
        summed = jnp.zeros((HD, HD), jnp.float32)
        for i in range(BLOCKS):
            summed = summed + parts[i, s * HD : (s + 1) * HD, :].astype(jnp.float32) * share[i]
        attn[:, pl.ds(pl.multiple_of(order[s] * HD, HD), HD)] = (
            (summed * (1.0 / total)).T.astype(jnp.bfloat16)
        )
    for s in range(FAR, GROUP):
        attn[:, pl.ds(pl.multiple_of(order[s] * HD, HD), HD)] = near[s - FAR]
    rows = attn[...]
    for i, copy in enumerate(copies):
        target = kept if i >= out.shape[0] else out
        copy.wait()
        target[i % out.shape[0]] = dot(rows, columns[i], NN).astype(target.dtype)


def add_kernel(kept, received, out):
    out[...] = (kept[...] + received[...].astype(jnp.float32)).astype(jnp.bfloat16)


def total_kernel(shares, out):
    total = shares[0].astype(jnp.float32)
    for i in range(1, shares.shape[0]):
        total = total + shares[i].astype(jnp.float32)
    out[...] = total.T.astype(jnp.bfloat16)


def call(kernel, outs, specs, scratch=(), vmem=24, flops=0, moved=0, exps=0):
    single = not isinstance(outs, list)
    return pl.pallas_call(
        kernel,
        out_shape=outs,
        in_specs=specs,
        out_specs=VMEM if single else [VMEM] * len(outs),
        scratch_shapes=list(scratch),
        compiler_params=pltpu.CompilerParams(vmem_limit_bytes=vmem * 2**20),
        cost_estimate=pl.CostEstimate(flops=flops, bytes_accessed=moved, transcendentals=exps),
    )


def per_device(queries, keys, values, cache_keys, cache_values, spans, out_weight):
    bf16, f32 = jnp.bfloat16, jnp.float32
    own, sent, near_rows = call(
        prepare_kernel,
        [
            jax.ShapeDtypeStruct((4 * HD, HD), bf16),
            jax.ShapeDtypeStruct((BLOCKS, FAR * HD, HD), bf16),
            jax.ShapeDtypeStruct((2 * HD, HD), bf16),
        ],
        [ANY] * 6,
        [
            pltpu.VMEM((HD, GROUP * HD), bf16),
            pltpu.SMEM((GROUP,), jnp.int32),
            pltpu.SemaphoreType.DMA((6,)),
        ],
        vmem=52,
        moved=2**21,
    )(spans, queries, keys, values, cache_keys, cache_values)
    grouped = lax.all_to_all(sent, ("e", "x"), 0, 0, tiled=True)
    up_route = [(i, (i + 1) % RING) for i in range(RING)]
    down_route = [(i, (i - 1) % RING) for i in range(RING)]
    kv, up, down = [own], own, own
    for _ in range(RING // 2 - 1):
        up = lax.ppermute(up, "k", up_route)
        down = lax.ppermute(down, "k", down_route)
        up, down = lax.optimization_barrier((up, down))
        kv += [up, down]
    last = lax.ppermute(up, "k", up_route)
    handed, held = call(
        hand_kernel,
        [
            jax.ShapeDtypeStruct((BLOCKS, 2 * HD, HD), bf16),
            jax.ShapeDtypeStruct((4 * HD, HD), bf16),
        ],
        [VMEM] * 2,
        moved=2**20,
    )(own, kv[1])
    kv[0] = held
    far_blocks = 2 * (RING - 1)
    state = call(
        first_kernel,
        [
            jax.ShapeDtypeStruct((TILES, HD + STATS, TILE), f32),
            jax.ShapeDtypeStruct((TILES, 8, TILE), f32),
        ],
        [SMEM] + [VMEM] * RING,
        [
            pltpu.VMEM((far_blocks * HD, HD), bf16),
            pltpu.VMEM((HD + STATS, far_blocks * HD), bf16),
            pltpu.VMEM((2, far_blocks * HD, TILE), f32),
        ],
        flops=4 * 2048 * 1792 * 128,
        moved=4 * 2**20,
        exps=2048 * 1792,
    )(spans, grouped, *kv)
    handed, last, state = lax.optimization_barrier((handed, last, state))
    blocks = lax.all_to_all(handed, ("e", "x"), 0, 0, tiled=True)
    partial = call(
        second_kernel,
        jax.ShapeDtypeStruct((BLOCKS, PIECE, HD), bf16),
        [SMEM] + [VMEM] * 4,
        [pltpu.VMEM((BLOCKS, STATS, HD), f32)],
        flops=4 * 2048 * 256 * 128,
        moved=4 * 2**20,
        exps=2048 * 256,
    )(spans, grouped, last, *state)
    parts = lax.all_to_all(partial, ("e", "x"), 0, 0, tiled=True)
    near = call(
        near_kernel,
        jax.ShapeDtypeStruct((2, HD, HD), bf16),
        [SMEM] + [VMEM] * 3,
        flops=4 * 256 * 640 * 128,
        moved=2**20,
        exps=256 * 640,
    )(spans, near_rows, held, blocks)
    width = out_weight.shape[1] // 8
    product, kept = call(
        project_kernel,
        [
            jax.ShapeDtypeStruct((4, HD, width), bf16),
            jax.ShapeDtypeStruct((4, HD, width), f32),
        ],
        [SMEM, VMEM, VMEM, ANY],
        [
            pltpu.VMEM((HD, GROUP * HD), bf16),
            pltpu.VMEM((8, GROUP * HD, width), bf16),
            pltpu.SemaphoreType.DMA((8,)),
        ],
        vmem=52,
        flops=2 * 128 * 512 * 4096,
        moved=5 * 2**20,
    )(spans, parts, near, out_weight)
    received = lax.ppermute(product, "c", [(0, 1), (1, 0)])
    halves = call(
        add_kernel,
        jax.ShapeDtypeStruct((4, HD, width), bf16),
        [VMEM] * 2,
        moved=2 * 2**20,
    )(kept, received)
    shares = lax.all_to_all(halves, "y", 0, 0, tiled=True)
    return call(
        total_kernel,
        jax.ShapeDtypeStruct((width, HD), bf16),
        [VMEM],
        moved=2**20,
    )(shares)


def solution(mesh):
    fine = Mesh(mesh.devices.reshape(RING, 2, 4, 4, 2), ("k", "e", "x", "y", "c"))
    seq, head = ("k", "e", "x"), ("y", "c")
    placed = (P(seq, head),) * 5 + (P(head), P(head, None))
    return jax.shard_map(
        per_device, mesh=fine, in_specs=placed, out_specs=P(head, seq), check_vma=False
    )
```

```python
import math

import jax
import jax.numpy as jnp
from jax import lax
from jax.experimental import pallas as pl
from jax.experimental.pallas import tpu as pltpu
from jax.sharding import Mesh
from jax.sharding import PartitionSpec as P

HD = 128
GROUP = 4
BLOCKS = 8
RING = 8
STATS = 16
PIECE = GROUP * HD + STATS
MASKED = -1e30
FLOOR = -1e29
FACTOR = math.log2(math.e) / math.sqrt(HD)
TILE = 2 * HD
TILES = 2 * BLOCKS * HD // TILE
CACHE = 2 * RING * BLOCKS // 2 * HD
VMEM = pl.BlockSpec(memory_space=pltpu.VMEM)
SMEM = pl.BlockSpec(memory_space=pltpu.SMEM)
ANY = pl.BlockSpec(memory_space=pl.ANY)
NT = (((1,), (1,)), ((), ()))
NN = (((1,), (0,)), ((), ()))


def dot(a, b, dims):
    return lax.dot_general(a, b, dims, preferred_element_type=jnp.float32)


def head_order(spans):
    far = [(spans[h] > 4 * HD).astype(jnp.int32) for h in range(GROUP)]
    order = [jnp.int32(0)] * GROUP
    ahead = jnp.int32(0)
    for h in range(GROUP):
        rank = jnp.where(far[h] == 1, ahead, 2 + h - ahead)
        ahead = ahead + far[h]
        order = [jnp.where(rank == s, h, order[s]) for s in range(GROUP)]
    return order


def prepare_kernel(
    spans, queries, keys, values, cache_keys, cache_values, own, sent, heads, kinds, sems
):
    copies = [
        pltpu.make_async_copy(spans, kinds, sems.at[0]),
        pltpu.make_async_copy(queries, heads, sems.at[1]),
    ]
    for i, source in enumerate([cache_keys, cache_values, keys, values]):
        copies.append(
            pltpu.make_async_copy(source, own.at[i * HD : (i + 1) * HD, :], sems.at[2 + i])
        )
    for copy in copies:
        copy.start()
    for copy in copies:
        copy.wait()
    order = head_order(kinds)
    for s in range(GROUP):
        rows = heads[:, pl.ds(pl.multiple_of(order[s] * HD, HD), HD)]
        for j in range(BLOCKS):
            sent[j, s] = rows


def position():
    return lax.axis_index("k"), lax.axis_index("e"), lax.axis_index("x")


def place(distance):
    k, e, x = position()
    return ((lax.rem(k + distance + RING, RING) * 2 + e) * 4 + x) * HD


def sources():
    first = jnp.where(lax.axis_index("c") == 0, -1, 1)
    return [0 * first, first, -first, 2 * first, -2 * first, 3 * first, -3 * first, 4 * first]


def offsets():
    token = lax.broadcasted_iota(jnp.int32, (HD, TILE), 1)
    return lax.rem(token, HD), token - lax.broadcasted_iota(jnp.int32, (HD, TILE), 0)


def tile_of(t):
    per = TILE // HD
    return t // (BLOCKS // per), t % (BLOCKS // per) * per


def masked_scores(spans, order, offset, key_rows, rows, t, cached, start):
    slot, first = tile_of(t)
    begin = CACHE + lax.axis_index("k") * (BLOCKS * HD) + first * HD
    found = dot(key_rows, rows, NT)
    if cached:
        allowed = offset < spans[order[slot]] - begin + start
    else:
        allowed = offset >= start + CACHE - begin
    return jnp.where(allowed, found, MASKED)


def highest(found):
    return jnp.max(found.reshape(HD // 8, 8, found.shape[1]), axis=0)


def first_kernel(spans, queries, *refs):
    kv = refs[: RING - 1]
    sums, tops, near, near_tops, keys, flipped, scores = refs[RING - 1 :]
    order = head_order(spans)
    distances = sources()
    blocks = []
    for i in range(RING - 1):
        for half in range(2):
            n = len(blocks)
            blocks.append((half == 0, place(distances[i])))
            keys[n * HD : (n + 1) * HD, :] = kv[i][2 * half * HD : (2 * half + 1) * HD, :]
            flipped[0:HD, n * HD : (n + 1) * HD] = kv[i][
                (2 * half + 1) * HD : (2 * half + 2) * HD, :
            ].T
    width = len(blocks) * HD
    flipped[HD:, :] = jnp.ones((STATS, width), jnp.bfloat16)
    column, offset = offsets()

    def score(t):
        slot, first = tile_of(t)
        rows = queries[first : first + TILE // HD, slot].reshape(TILE, HD)
        top = jnp.full((8, TILE), FLOOR, jnp.float32)
        for n, (cached, start) in enumerate(blocks):
            found = masked_scores(
                spans, order, offset, keys[n * HD : (n + 1) * HD, :], rows, t, cached, start
            )
            scores[t % 2, n * HD : (n + 1) * HD, :] = found
            top = jnp.maximum(top, highest(found))
        return jnp.max(top, axis=0, keepdims=True)

    def finish(t, top):
        weights = jnp.concatenate(
            [
                jnp.exp2((scores[t % 2, n * HD : (n + 1) * HD, :] - top) * FACTOR).astype(
                    jnp.bfloat16
                )
                for n in range(len(blocks))
            ],
            axis=0,
        )
        sums[t] = dot(flipped[...], weights, NN)
        tops[t] = jnp.broadcast_to(top, (8, TILE))

    k, e, x = position()
    own = e * 4 + x
    wraps = k == 0
    n = jnp.where(lax.axis_index("c") == 0, 2, 4) + jnp.where(wraps, 0, 1)
    at = pl.multiple_of(n * HD, HD)
    before_keys = keys[pl.ds(at, HD), :]
    before_values = flipped[:, pl.ds(at, HD)]
    before_start = place(-1) + jnp.where(wraps, 0, CACHE)
    own_start = place(0) + CACHE
    span = jnp.where(
        lax.broadcasted_iota(jnp.int32, (HD, TILE), 1) < HD, spans[order[2]], spans[order[3]]
    )
    near_offset = column - lax.broadcasted_iota(jnp.int32, (HD, TILE), 0)
    for b in range(BLOCKS):
        earlier = b < own
        rows = queries[b, 2:4].reshape(TILE, HD)
        found = dot(jnp.where(earlier, before_keys, keys[HD : 2 * HD, :]), rows, NT)
        begin = CACHE + (k * BLOCKS + b) * HD
        behind = near_offset + (begin - jnp.where(earlier, before_start, own_start))
        found = jnp.where((behind >= 0) & (behind < span), found, MASKED)
        top = jnp.maximum(jnp.max(found, axis=0, keepdims=True), FLOOR)
        weights = jnp.exp2((found - top) * FACTOR).astype(jnp.bfloat16)
        near[b] = dot(jnp.where(earlier, before_values, flipped[:, HD : 2 * HD]), weights, NN)
        near_tops[b] = jnp.broadcast_to(top, (8, TILE))

    top = score(0)
    for t in range(TILES):
        later = score(t + 1) if t + 1 < TILES else None
        finish(t, top)
        top = later


def write_stats(stats, block, slot, top, total):
    level = jnp.where(total > 0.0, top * FACTOR + jnp.log2(total), MASKED)
    for i in range(3):
        term = level.astype(jnp.bfloat16).astype(jnp.float32)
        stats[block, slot * 4 + i : slot * 4 + i + 1, :] = term
        level = level - term


def second_kernel(spans, queries, last, sums, tops, near, near_tops, out, stats):
    order = head_order(spans)
    start = place(sources()[-1])
    _, offset = offsets()
    ones = jnp.ones((STATS, HD), jnp.bfloat16)
    flipped = jnp.concatenate(
        [
            jnp.concatenate([last[HD : 2 * HD, :].T, ones], axis=0),
            jnp.concatenate([last[3 * HD :, :].T, ones], axis=0),
        ],
        axis=1,
    )
    stats[...] = jnp.zeros_like(stats)

    def emit(block, slot, top, summed):
        total = summed[HD : HD + 1, :]
        normal = summed[:HD, :] * (1.0 / jnp.maximum(total, 1e-30))
        out[block, slot * HD : (slot + 1) * HD, :] = normal.astype(jnp.bfloat16)
        write_stats(stats, block, slot, top, total)

    for b in range(BLOCKS):
        for j in range(2):
            cut = slice(j * HD, (j + 1) * HD)
            emit(b, 2 + j, near_tops[b, 0:1, cut], near[b, :, cut])
    for t in range(TILES):
        slot, first = tile_of(t)
        rows = queries[first : first + TILE // HD, slot].reshape(TILE, HD)
        found = [
            masked_scores(
                spans, order, offset, last[2 * half * HD : (2 * half + 1) * HD, :],
                rows, t, half == 0, start,
            )
            for half in range(2)
        ]
        before = tops[t, 0:1, :]
        top = jnp.max(jnp.maximum(highest(found[0]), highest(found[1])), axis=0, keepdims=True)
        top = jnp.maximum(top, before)
        weights = [jnp.exp2((f - top) * FACTOR).astype(jnp.bfloat16) for f in found]
        summed = sums[t] * jnp.exp2((before - top) * FACTOR) + dot(
            flipped, jnp.concatenate(weights, axis=0), NN
        )
        for j in range(TILE // HD):
            cut = slice(j * HD, (j + 1) * HD)
            emit(first + j, slot, top[:, cut], summed[:, cut])
    out[:, GROUP * HD :, :] = stats[...].astype(jnp.bfloat16)


def project_kernel(spans, parts, weight, out, kept, attn):
    order = head_order(spans)
    for s in range(GROUP):
        terms = parts[:, GROUP * HD :, :].astype(jnp.float32)
        level = [
            terms[i, 4 * s : 4 * s + 1] + terms[i, 4 * s + 1 : 4 * s + 2] + terms[i, 4 * s + 2 : 4 * s + 3]
            for i in range(BLOCKS)
        ]
        top = level[0]
        for i in range(1, BLOCKS):
            top = jnp.maximum(top, level[i])
        share = [jnp.exp2(v - top) for v in level]
        total = share[0]
        for i in range(1, BLOCKS):
            total = total + share[i]
        summed = jnp.zeros((HD, HD), jnp.float32)
        for i in range(BLOCKS):
            summed = summed + parts[i, s * HD : (s + 1) * HD, :].astype(jnp.float32) * share[i]
        attn[:, pl.ds(pl.multiple_of(order[s] * HD, HD), HD)] = (
            (summed * (1.0 / total)).T.astype(jnp.bfloat16)
        )
    rows = attn[...]
    mine = lax.axis_index("c")
    width = out.shape[2]
    for core, target in ((1 - mine, out), (mine, kept)):
        for f in range(out.shape[0]):
            at = pl.multiple_of((2 * f + core) * width, width)
            product = dot(rows, weight[:, pl.ds(at, width)], NN)
            target[f] = product.astype(target.dtype)


def add_kernel(kept, received, out):
    out[...] = (kept[...] + received[...].astype(jnp.float32)).astype(jnp.bfloat16)


def total_kernel(shares, out):
    total = shares[0].astype(jnp.float32)
    for i in range(1, shares.shape[0]):
        total = total + shares[i].astype(jnp.float32)
    out[...] = total.T.astype(jnp.bfloat16)


def call(kernel, outs, specs, scratch=(), vmem=24, flops=0, moved=0, exps=0):
    single = not isinstance(outs, list)
    return pl.pallas_call(
        kernel,
        out_shape=outs,
        in_specs=specs,
        out_specs=VMEM if single else [VMEM] * len(outs),
        scratch_shapes=list(scratch),
        compiler_params=pltpu.CompilerParams(vmem_limit_bytes=vmem * 2**20),
        cost_estimate=pl.CostEstimate(flops=flops, bytes_accessed=moved, transcendentals=exps),
    )


def per_device(queries, keys, values, cache_keys, cache_values, spans, out_weight):
    bf16, f32 = jnp.bfloat16, jnp.float32
    own, sent = call(
        prepare_kernel,
        [
            jax.ShapeDtypeStruct((4 * HD, HD), bf16),
            jax.ShapeDtypeStruct((BLOCKS, GROUP, HD, HD), bf16),
        ],
        [ANY] * 6,
        [
            pltpu.VMEM((HD, GROUP * HD), bf16),
            pltpu.SMEM((GROUP,), jnp.int32),
            pltpu.SemaphoreType.DMA((6,)),
        ],
        vmem=60,
        moved=2**21,
    )(spans, queries, keys, values, cache_keys, cache_values)
    routes = [
        [
            (2 * i + c, (i + (1 if c == turn else -1)) % RING * 2 + c)
            for i in range(RING)
            for c in range(2)
        ]
        for turn in range(2)
    ]
    kv, one, two = [own], own, own
    for _ in range(RING // 2 - 1):
        one = lax.ppermute(one, ("k", "c"), routes[0])
        two = lax.ppermute(two, ("k", "c"), routes[1])
        kv += [one, two]
    last = lax.ppermute(one, ("k", "c"), routes[0])
    grouped = lax.all_to_all(sent, ("e", "x"), 0, 0, tiled=True)

    near_blocks = 2 * (RING - 1)
    state = call(
        first_kernel,
        [
            jax.ShapeDtypeStruct((TILES, HD + STATS, TILE), f32),
            jax.ShapeDtypeStruct((TILES, 8, TILE), f32),
            jax.ShapeDtypeStruct((BLOCKS, HD + STATS, TILE), f32),
            jax.ShapeDtypeStruct((BLOCKS, 8, TILE), f32),
        ],
        [SMEM] + [VMEM] * RING,
        [
            pltpu.VMEM((near_blocks * HD, HD), bf16),
            pltpu.VMEM((HD + STATS, near_blocks * HD), bf16),
            pltpu.VMEM((2, near_blocks * HD, TILE), f32),
        ],
        flops=4 * 2048 * 1792 * 128,
        moved=4 * 2**20,
        exps=2048 * 1792,
    )(spans, grouped, *kv)
    partial = call(
        second_kernel,
        jax.ShapeDtypeStruct((BLOCKS, PIECE, HD), bf16),
        [SMEM] + [VMEM] * 6,
        [pltpu.VMEM((BLOCKS, STATS, HD), f32)],
        flops=4 * 2048 * 256 * 128,
        moved=4 * 2**20,
        exps=2048 * 256,
    )(spans, grouped, last, *state)
    parts = lax.all_to_all(partial, ("e", "x"), 0, 0, tiled=True)
    width = out_weight.shape[1] // 8
    product, kept = call(
        project_kernel,
        [
            jax.ShapeDtypeStruct((4, HD, width), bf16),
            jax.ShapeDtypeStruct((4, HD, width), f32),
        ],
        [SMEM, VMEM, VMEM],
        [pltpu.VMEM((HD, GROUP * HD), bf16)],
        flops=2 * 128 * 512 * 4096,
        moved=5 * 2**20,
    )(spans, parts, out_weight)
    received = lax.ppermute(product, "c", [(0, 1), (1, 0)])
    halves = call(
        add_kernel,
        jax.ShapeDtypeStruct((4, HD, width), bf16),
        [VMEM] * 2,
        moved=2 * 2**20,
    )(kept, received)
    shares = lax.all_to_all(halves, "y", 0, 0, tiled=True)
    return call(
        total_kernel,
        jax.ShapeDtypeStruct((width, HD), bf16),
        [VMEM],
        moved=2**20,
    )(shares)


def solution(mesh):
    fine = Mesh(mesh.devices.reshape(RING, 2, 4, 4, 2), ("k", "e", "x", "y", "c"))
    seq, head = ("k", "e", "x"), ("y", "c")
    placed = (P(seq, head),) * 5 + (P(head), P(head, None))
    return jax.shard_map(
        per_device, mesh=fine, in_specs=placed, out_specs=P(head, seq), check_vma=False
    )
```

```python
import math

import jax
import jax.numpy as jnp
from jax import lax
from jax.experimental import pallas as pl
from jax.experimental.pallas import tpu as pltpu
from jax.sharding import Mesh
from jax.sharding import PartitionSpec as P

HD = 128
GROUP = 4
FAR = 2
BLOCKS = 8
RING = 8
STATS = 16
PIECE = FAR * HD + STATS
MASKED = -1e30
FLOOR = -1e29
FACTOR = math.log2(math.e) / math.sqrt(HD)
TILE = 2 * HD
TILES = 2 * BLOCKS * HD // TILE
CACHE = 2 * RING * BLOCKS // 2 * HD
VMEM = pl.BlockSpec(memory_space=pltpu.VMEM)
SMEM = pl.BlockSpec(memory_space=pltpu.SMEM)
ANY = pl.BlockSpec(memory_space=pl.ANY)
NT = (((1,), (1,)), ((), ()))
NN = (((1,), (0,)), ((), ()))


def dot(a, b, dims):
    return lax.dot_general(a, b, dims, preferred_element_type=jnp.float32)


def head_order(spans):
    far = [(spans[h] > 4 * HD).astype(jnp.int32) for h in range(GROUP)]
    order = [jnp.int32(0)] * GROUP
    ahead = jnp.int32(0)
    for h in range(GROUP):
        rank = jnp.where(far[h] == 1, ahead, 2 + h - ahead)
        ahead = ahead + far[h]
        order = [jnp.where(rank == s, h, order[s]) for s in range(GROUP)]
    return order


def prepare_kernel(
    spans, queries, keys, values, cache_keys, cache_values, own, far_rows, near_rows, handed, heads, kinds, sems
):
    copies = [
        pltpu.make_async_copy(spans, kinds, sems.at[0]),
        pltpu.make_async_copy(queries, heads, sems.at[1]),
    ]
    for i, source in enumerate([cache_keys, cache_values, keys, values]):
        copies.append(
            pltpu.make_async_copy(source, own.at[i * HD : (i + 1) * HD, :], sems.at[2 + i])
        )
    for copy in copies:
        copy.start()
    for copy in copies:
        copy.wait()
    k, e, _ = position()
    ends = (k == RING - 1) & (e == 1)
    handed[...] = jnp.where(ends, own[: 2 * HD, :], own[2 * HD :, :])
    order = head_order(kinds)
    for s in range(GROUP):
        rows = heads[:, pl.ds(pl.multiple_of(order[s] * HD, HD), HD)]
        target = far_rows if s < FAR else near_rows
        target[s % FAR * HD : (s % FAR + 1) * HD, :] = rows


def spread_kernel(far_rows, other_rows, own, prior, after, after_too, sent):
    del after, after_too
    first = lax.axis_index("e") == 0
    lower = jnp.where(first, far_rows[...], other_rows[...])
    upper = jnp.where(first, other_rows[...], far_rows[...])
    for j in range(4):
        sent[j, : 2 * HD, :] = lower
        sent[j, 2 * HD : 4 * HD, :] = upper
        sent[j, 4 * HD : 6 * HD, :] = own[2 * HD :, :]
        sent[j, 6 * HD :, :] = prior[...]


def query_rows(gathered, slot, first):
    at = first // 4 * 2 * HD + slot * HD
    return gathered[first % 4 : first % 4 + TILE // HD, at : at + HD, :].reshape(TILE, HD)


def position():
    return lax.axis_index("k"), lax.axis_index("e"), lax.axis_index("x")


def place(distance):
    k, e, x = position()
    return ((lax.rem(k + distance + RING, RING) * 2 + e) * 4 + x) * HD


def sources():
    first = jnp.where(lax.axis_index("c") == 0, -1, 1)
    return [0 * first, first, -first, 2 * first, -2 * first, 3 * first, -3 * first, 4 * first]


def offsets():
    token = lax.broadcasted_iota(jnp.int32, (HD, TILE), 1)
    return lax.rem(token, HD), token - lax.broadcasted_iota(jnp.int32, (HD, TILE), 0)


def tile_of(t):
    per = TILE // HD
    return t // (BLOCKS // per), t % (BLOCKS // per) * per


def masked_scores(spans, order, offset, key_rows, rows, t, cached, start):
    slot, first = tile_of(t)
    begin = CACHE + lax.axis_index("k") * (BLOCKS * HD) + first * HD
    found = dot(key_rows, rows, NT)
    if cached:
        allowed = offset < spans[order[slot]] - begin + start
    else:
        allowed = offset >= start + CACHE - begin
    return jnp.where(allowed, found, MASKED)


def highest(found):
    return jnp.max(found.reshape(HD // 8, 8, found.shape[1]), axis=0)


def first_kernel(spans, queries, *refs):
    kv = refs[: RING - 1]
    sums, tops, keys, flipped, scores = refs[RING - 1 :]
    order = head_order(spans)
    distances = sources()
    blocks = []
    for i in range(RING - 1):
        for half in range(2):
            n = len(blocks)
            blocks.append((half == 0, place(distances[i])))
            keys[n * HD : (n + 1) * HD, :] = kv[i][2 * half * HD : (2 * half + 1) * HD, :]
            flipped[0:HD, n * HD : (n + 1) * HD] = kv[i][
                (2 * half + 1) * HD : (2 * half + 2) * HD, :
            ].T
    width = len(blocks) * HD
    flipped[HD:, :] = jnp.ones((STATS, width), jnp.bfloat16)
    _, offset = offsets()

    def score(t):
        slot, first = tile_of(t)
        rows = query_rows(queries, slot, first)
        top = jnp.full((8, TILE), FLOOR, jnp.float32)
        for n, (cached, start) in enumerate(blocks):
            found = masked_scores(
                spans, order, offset, keys[n * HD : (n + 1) * HD, :], rows, t, cached, start
            )
            scores[t % 2, n * HD : (n + 1) * HD, :] = found
            top = jnp.maximum(top, highest(found))
        return jnp.max(top, axis=0, keepdims=True)

    def finish(t, top):
        weights = jnp.concatenate(
            [
                jnp.exp2((scores[t % 2, n * HD : (n + 1) * HD, :] - top) * FACTOR).astype(
                    jnp.bfloat16
                )
                for n in range(len(blocks))
            ],
            axis=0,
        )
        sums[t] = dot(flipped[...], weights, NN)
        tops[t] = jnp.broadcast_to(top, (8, TILE))

    top = score(0)
    for t in range(TILES):
        later = score(t + 1) if t + 1 < TILES else None
        finish(t, top)
        top = later


def near_kernel(spans, rows, own, gathered, out):
    order = head_order(spans)
    x = lax.axis_index("x")
    column, _ = offsets()
    behind = column - lax.broadcasted_iota(jnp.int32, (HD, TILE), 0)
    span = jnp.where(
        lax.broadcasted_iota(jnp.int32, (HD, TILE), 1) < HD, spans[order[2]], spans[order[3]]
    )
    found, values = [], []
    for j in range(5):
        if j < 4:
            distance = jnp.where(j < x, x - j, x - j + 4) * HD
            block = jnp.where(j < x, gathered[j, 4 * HD : 6 * HD, :], gathered[j, 6 * HD :, :])
            key_rows, value_rows = block[:HD, :], block[HD:, :]
        else:
            distance = 0
            key_rows, value_rows = own[2 * HD : 3 * HD, :], own[3 * HD :, :]
        far = behind + distance
        found.append(
            jnp.where((far >= 0) & (far < span), dot(key_rows, rows[...], NT), MASKED)
        )
        values.append(value_rows)
    top = highest(found[0])
    for j in range(1, 5):
        top = jnp.maximum(top, highest(found[j]))
    top = jnp.max(top, axis=0, keepdims=True)
    weights = jnp.concatenate(
        [jnp.exp2((f - top) * FACTOR).astype(jnp.bfloat16) for f in found], axis=0
    )
    flipped = jnp.concatenate([v.T for v in values], axis=1)
    flipped = jnp.concatenate([flipped, jnp.ones((STATS, 5 * HD), jnp.bfloat16)], axis=0)
    summed = dot(flipped, weights, NN)
    normal = summed[:HD, :] * (1.0 / summed[HD : HD + 1, :])
    for s in range(2):
        out[s] = normal[:, s * HD : (s + 1) * HD].T.astype(jnp.bfloat16)


def write_stats(stats, block, slot, top, total):
    level = jnp.where(total > 0.0, top * FACTOR + jnp.log2(total), MASKED)
    for i in range(3):
        term = level.astype(jnp.bfloat16).astype(jnp.float32)
        stats[block, slot * 4 + i : slot * 4 + i + 1, :] = term
        level = level - term


def second_kernel(spans, queries, last, sums, tops, after, out, stats):
    del after
    order = head_order(spans)
    start = place(sources()[-1])
    _, offset = offsets()
    ones = jnp.ones((STATS, HD), jnp.bfloat16)
    flipped = jnp.concatenate(
        [
            jnp.concatenate([last[HD : 2 * HD, :].T, ones], axis=0),
            jnp.concatenate([last[3 * HD :, :].T, ones], axis=0),
        ],
        axis=1,
    )
    stats[...] = jnp.zeros_like(stats)
    for t in range(TILES):
        slot, first = tile_of(t)
        rows = query_rows(queries, slot, first)
        found = [
            masked_scores(
                spans, order, offset, last[2 * half * HD : (2 * half + 1) * HD, :],
                rows, t, half == 0, start,
            )
            for half in range(2)
        ]
        before = tops[t, 0:1, :]
        top = jnp.max(jnp.maximum(highest(found[0]), highest(found[1])), axis=0, keepdims=True)
        top = jnp.maximum(top, before)
        weights = [jnp.exp2((f - top) * FACTOR).astype(jnp.bfloat16) for f in found]
        summed = sums[t] * jnp.exp2((before - top) * FACTOR) + dot(
            flipped, jnp.concatenate(weights, axis=0), NN
        )
        total = summed[HD : HD + 1, :]
        normal = summed[:HD, :] * (1.0 / jnp.maximum(total, 1e-30))
        for j in range(TILE // HD):
            cut = slice(j * HD, (j + 1) * HD)
            out[first + j, slot * HD : (slot + 1) * HD, :] = normal[:, cut].astype(jnp.bfloat16)
            write_stats(stats, first + j, slot, top[:, cut], total[:, cut])
    out[:, FAR * HD :, :] = stats[...].astype(jnp.bfloat16)


def project_kernel(spans, parts, near, weight, out, kept, attn):
    order = head_order(spans)
    terms = parts[:, FAR * HD :, :].astype(jnp.float32)
    for s in range(FAR):
        level = [
            terms[i, 4 * s : 4 * s + 1] + terms[i, 4 * s + 1 : 4 * s + 2] + terms[i, 4 * s + 2 : 4 * s + 3]
            for i in range(BLOCKS)
        ]
        top = level[0]
        for i in range(1, BLOCKS):
            top = jnp.maximum(top, level[i])
        share = [jnp.exp2(v - top) for v in level]
        total = share[0]
        for i in range(1, BLOCKS):
            total = total + share[i]
        summed = jnp.zeros((HD, HD), jnp.float32)
        for i in range(BLOCKS):
            summed = summed + parts[i, s * HD : (s + 1) * HD, :].astype(jnp.float32) * share[i]
        attn[:, pl.ds(pl.multiple_of(order[s] * HD, HD), HD)] = (
            (summed * (1.0 / total)).T.astype(jnp.bfloat16)
        )
    for s in range(FAR, GROUP):
        attn[:, pl.ds(pl.multiple_of(order[s] * HD, HD), HD)] = near[s - FAR]
    rows = attn[...]
    mine = lax.axis_index("c")
    width = out.shape[2]
    for core, target in ((1 - mine, out), (mine, kept)):
        for f in range(out.shape[0]):
            at = pl.multiple_of((2 * f + core) * width, width)
            product = dot(rows, weight[:, pl.ds(at, width)], NN)
            target[f] = product.astype(target.dtype)


def add_kernel(kept, received, out):
    out[...] = (kept[...] + received[...].astype(jnp.float32)).astype(jnp.bfloat16)


def total_kernel(shares, out):
    total = shares[0].astype(jnp.float32)
    for i in range(1, shares.shape[0]):
        total = total + shares[i].astype(jnp.float32)
    out[...] = total.T.astype(jnp.bfloat16)


def call(kernel, outs, specs, scratch=(), vmem=24, flops=0, moved=0, exps=0):
    single = not isinstance(outs, list)
    return pl.pallas_call(
        kernel,
        out_shape=outs,
        in_specs=specs,
        out_specs=VMEM if single else [VMEM] * len(outs),
        scratch_shapes=list(scratch),
        compiler_params=pltpu.CompilerParams(vmem_limit_bytes=vmem * 2**20),
        cost_estimate=pl.CostEstimate(flops=flops, bytes_accessed=moved, transcendentals=exps),
    )


def per_device(queries, keys, values, cache_keys, cache_values, spans, out_weight):
    bf16, f32 = jnp.bfloat16, jnp.float32
    own, far_rows, near_rows, handed = call(
        prepare_kernel,
        [
            jax.ShapeDtypeStruct((4 * HD, HD), bf16),
            jax.ShapeDtypeStruct((FAR * HD, HD), bf16),
            jax.ShapeDtypeStruct((FAR * HD, HD), bf16),
            jax.ShapeDtypeStruct((2 * HD, HD), bf16),
        ],
        [ANY] * 6,
        [
            pltpu.VMEM((HD, GROUP * HD), bf16),
            pltpu.SMEM((GROUP,), jnp.int32),
            pltpu.SemaphoreType.DMA((6,)),
        ],
        vmem=60,
        moved=2**20,
    )(spans, queries, keys, values, cache_keys, cache_values)
    other_rows = lax.ppermute(far_rows, "e", [(0, 1), (1, 0)])
    prior = lax.ppermute(
        handed, ("k", "e"), [(i, (i + 1) % (2 * RING)) for i in range(2 * RING)]
    )
    routes = [
        [
            (2 * i + c, (i + (1 if c == turn else -1)) % RING * 2 + c)
            for i in range(RING)
            for c in range(2)
        ]
        for turn in range(2)
    ]
    kv, one, two = [own], own, own
    for _ in range(RING // 2 - 1):
        one = lax.ppermute(one, ("k", "c"), routes[0])
        two = lax.ppermute(two, ("k", "c"), routes[1])
        kv += [one, two]
    last = lax.ppermute(one, ("k", "c"), routes[0])
    sent = call(
        spread_kernel,
        jax.ShapeDtypeStruct((4, 8 * HD, HD), bf16),
        [VMEM] * 4 + [ANY] * 2,
        moved=2**20,
    )(far_rows, other_rows, own, prior, kv[3], kv[4])
    grouped = lax.all_to_all(sent, "x", 0, 0, tiled=True)
    near = call(
        near_kernel,
        jax.ShapeDtypeStruct((2, HD, HD), bf16),
        [SMEM] + [VMEM] * 3,
        flops=4 * 256 * 640 * 128,
        moved=2**20,
        exps=256 * 640,
    )(spans, near_rows, own, grouped)

    near_blocks = 2 * (RING - 1)
    state = call(
        first_kernel,
        [
            jax.ShapeDtypeStruct((TILES, HD + STATS, TILE), f32),
            jax.ShapeDtypeStruct((TILES, 8, TILE), f32),
        ],
        [SMEM] + [VMEM] * RING,
        [
            pltpu.VMEM((near_blocks * HD, HD), bf16),
            pltpu.VMEM((HD + STATS, near_blocks * HD), bf16),
            pltpu.VMEM((2, near_blocks * HD, TILE), f32),
        ],
        flops=4 * 2048 * 1792 * 128,
        moved=4 * 2**20,
        exps=2048 * 1792,
    )(spans, grouped, *kv)
    partial = call(
        second_kernel,
        jax.ShapeDtypeStruct((BLOCKS, PIECE, HD), bf16),
        [SMEM] + [VMEM] * 4 + [ANY],
        [pltpu.VMEM((BLOCKS, STATS, HD), f32)],
        flops=4 * 2048 * 256 * 128,
        moved=4 * 2**20,
        exps=2048 * 256,
    )(spans, grouped, last, *state, near)
    parts = lax.all_to_all(partial, ("e", "x"), 0, 0, tiled=True)
    width = out_weight.shape[1] // 8
    product, kept = call(
        project_kernel,
        [
            jax.ShapeDtypeStruct((4, HD, width), bf16),
            jax.ShapeDtypeStruct((4, HD, width), f32),
        ],
        [SMEM, VMEM, VMEM, VMEM],
        [pltpu.VMEM((HD, GROUP * HD), bf16)],
        flops=2 * 128 * 512 * 4096,
        moved=5 * 2**20,
    )(spans, parts, near, out_weight)
    received = lax.ppermute(product, "c", [(0, 1), (1, 0)])
    halves = call(
        add_kernel,
        jax.ShapeDtypeStruct((4, HD, width), bf16),
        [VMEM] * 2,
        moved=2 * 2**20,
    )(kept, received)
    shares = lax.all_to_all(halves, "y", 0, 0, tiled=True)
    return call(
        total_kernel,
        jax.ShapeDtypeStruct((width, HD), bf16),
        [VMEM],
        moved=2**20,
    )(shares)


def solution(mesh):
    fine = Mesh(mesh.devices.reshape(RING, 2, 4, 4, 2), ("k", "e", "x", "y", "c"))
    seq, head = ("k", "e", "x"), ("y", "c")
    placed = (P(seq, head),) * 5 + (P(head), P(head, None))
    return jax.shard_map(
        per_device, mesh=fine, in_specs=placed, out_specs=P(head, seq), check_vma=False
    )
```

```python
import math

import jax
import jax.numpy as jnp
from jax import lax
from jax.experimental import pallas as pl
from jax.experimental.pallas import tpu as pltpu
from jax.sharding import Mesh
from jax.sharding import PartitionSpec as P

HD = 128
GROUP = 4
FAR = 2
BLOCKS = 8
RING = 8
STATS = 16
PIECE = FAR * HD + STATS
MASKED = -1e30
FLOOR = -1e29
FACTOR = math.log2(math.e) / math.sqrt(HD)
TILE = 2 * HD
TILES = 2 * BLOCKS * HD // TILE
CACHE = 2 * RING * BLOCKS // 2 * HD
VMEM = pl.BlockSpec(memory_space=pltpu.VMEM)
SMEM = pl.BlockSpec(memory_space=pltpu.SMEM)
ANY = pl.BlockSpec(memory_space=pl.ANY)
NT = (((1,), (1,)), ((), ()))
NN = (((1,), (0,)), ((), ()))


def dot(a, b, dims):
    return lax.dot_general(a, b, dims, preferred_element_type=jnp.float32)


def head_order(spans):
    far = [(spans[h] > 4 * HD).astype(jnp.int32) for h in range(GROUP)]
    order = [jnp.int32(0)] * GROUP
    ahead = jnp.int32(0)
    for h in range(GROUP):
        rank = jnp.where(far[h] == 1, ahead, 2 + h - ahead)
        ahead = ahead + far[h]
        order = [jnp.where(rank == s, h, order[s]) for s in range(GROUP)]
    return order


def prepare_kernel(
    spans, queries, keys, values, cache_keys, cache_values, own, own_rows, heads, kinds, sems
):
    copies = [
        pltpu.make_async_copy(spans, kinds, sems.at[0]),
        pltpu.make_async_copy(queries, heads, sems.at[1]),
    ]
    for i, source in enumerate([cache_keys, cache_values, keys, values]):
        copies.append(
            pltpu.make_async_copy(source, own.at[i * HD : (i + 1) * HD, :], sems.at[2 + i])
        )
    for copy in copies:
        copy.start()
    for copy in copies:
        copy.wait()
    order = head_order(kinds)
    for s in range(GROUP):
        rows = heads[:, pl.ds(pl.multiple_of(order[s] * HD, HD), HD)]
        own_rows[s * HD : (s + 1) * HD, :] = rows


def hand_kernel(own_rows, own, one, two, sent, held, near_rows):
    k, e, x = position()
    me = e * 4 + x
    below = jnp.where(lax.axis_index("c") == 0, one[...], two[...])
    prior = jnp.where(k == 0, below[: 2 * HD, :], below[2 * HD :, :])
    block = own[2 * HD :, :]
    rows = own_rows[: FAR * HD, :]
    near_rows[...] = own_rows[FAR * HD :, :]
    held[...] = own[...]
    for j in range(BLOCKS):
        sent[j, : FAR * HD, :] = rows
        sent[j, FAR * HD :, :] = jnp.where(j >= me, block, prior)


def query_rows(grouped, slot, first):
    at = slot * HD
    return grouped[first : first + TILE // HD, at : at + HD, :].reshape(TILE, HD)


def position():
    return lax.axis_index("k"), lax.axis_index("e"), lax.axis_index("x")


def place(distance):
    k, e, x = position()
    return ((lax.rem(k + distance + RING, RING) * 2 + e) * 4 + x) * HD


def sources():
    first = jnp.where(lax.axis_index("c") == 0, -1, 1)
    return [0 * first, first, -first, 2 * first, -2 * first, 3 * first, -3 * first, 4 * first]


def offsets():
    token = lax.broadcasted_iota(jnp.int32, (HD, TILE), 1)
    return lax.rem(token, HD), token - lax.broadcasted_iota(jnp.int32, (HD, TILE), 0)


def tile_of(t):
    per = TILE // HD
    return t // (BLOCKS // per), t % (BLOCKS // per) * per


def masked_scores(spans, order, offset, key_rows, rows, t, cached, start):
    slot, first = tile_of(t)
    begin = CACHE + lax.axis_index("k") * (BLOCKS * HD) + first * HD
    found = dot(key_rows, rows, NT)
    if cached:
        allowed = offset < spans[order[slot]] - begin + start
    else:
        allowed = offset >= start + CACHE - begin
    return jnp.where(allowed, found, MASKED)


def highest(found):
    return jnp.max(found.reshape(HD // 8, 8, found.shape[1]), axis=0)


def near_heads(spans, order, rows, grouped, out):
    _, e, x = position()
    me = e * 4 + x
    column, _ = offsets()
    behind = column - lax.broadcasted_iota(jnp.int32, (HD, TILE), 0)
    span = jnp.where(
        lax.broadcasted_iota(jnp.int32, (HD, TILE), 1) < HD, spans[order[2]], spans[order[3]]
    )
    found, values = [], []
    for j in range(5):
        block = grouped[lax.rem(me - j + BLOCKS, BLOCKS), FAR * HD :, :]
        far = behind + j * HD
        found.append(
            jnp.where((far >= 0) & (far < span), dot(block[:HD, :], rows[...], NT), MASKED)
        )
        values.append(block[HD:, :])
    top = highest(found[0])
    for j in range(1, 5):
        top = jnp.maximum(top, highest(found[j]))
    top = jnp.max(top, axis=0, keepdims=True)
    weights = jnp.concatenate(
        [jnp.exp2((f - top) * FACTOR).astype(jnp.bfloat16) for f in found], axis=0
    )
    flipped = jnp.concatenate([v.T for v in values], axis=1)
    flipped = jnp.concatenate([flipped, jnp.ones((STATS, 5 * HD), jnp.bfloat16)], axis=0)
    summed = dot(flipped, weights, NN)
    normal = summed[:HD, :] * (1.0 / summed[HD : HD + 1, :])
    for s in range(2):
        out[s] = normal[:, s * HD : (s + 1) * HD].T.astype(jnp.bfloat16)


def first_kernel(spans, near_rows, queries, *refs):
    kv = refs[: RING - 1]
    sums, tops, near, keys, flipped, scores = refs[RING - 1 :]
    order = head_order(spans)
    distances = sources()
    blocks = []
    for i in range(RING - 1):
        for half in range(2):
            n = len(blocks)
            blocks.append((half == 0, place(distances[i])))
            keys[n * HD : (n + 1) * HD, :] = kv[i][2 * half * HD : (2 * half + 1) * HD, :]
            flipped[0:HD, n * HD : (n + 1) * HD] = kv[i][
                (2 * half + 1) * HD : (2 * half + 2) * HD, :
            ].T
    width = len(blocks) * HD
    flipped[HD:, :] = jnp.ones((STATS, width), jnp.bfloat16)
    _, offset = offsets()

    def score(t):
        slot, first = tile_of(t)
        rows = query_rows(queries, slot, first)
        top = jnp.full((8, TILE), FLOOR, jnp.float32)
        for n, (cached, start) in enumerate(blocks):
            found = masked_scores(
                spans, order, offset, keys[n * HD : (n + 1) * HD, :], rows, t, cached, start
            )
            scores[t % 2, n * HD : (n + 1) * HD, :] = found
            top = jnp.maximum(top, highest(found))
        return jnp.max(top, axis=0, keepdims=True)

    def finish(t, top):
        weights = jnp.concatenate(
            [
                jnp.exp2((scores[t % 2, n * HD : (n + 1) * HD, :] - top) * FACTOR).astype(
                    jnp.bfloat16
                )
                for n in range(len(blocks))
            ],
            axis=0,
        )
        sums[t] = dot(flipped[...], weights, NN)
        tops[t] = jnp.broadcast_to(top, (8, TILE))

    near_heads(spans, order, near_rows, queries, near)
    top = score(0)
    for t in range(TILES):
        later = score(t + 1) if t + 1 < TILES else None
        finish(t, top)
        top = later


def write_stats(stats, block, slot, top, total):
    level = jnp.where(total > 0.0, top * FACTOR + jnp.log2(total), MASKED)
    for i in range(3):
        term = level.astype(jnp.bfloat16).astype(jnp.float32)
        stats[block, slot * 4 + i : slot * 4 + i + 1, :] = term
        level = level - term


def second_kernel(spans, queries, last, sums, tops, out, stats):
    order = head_order(spans)
    start = place(sources()[-1])
    _, offset = offsets()
    ones = jnp.ones((STATS, HD), jnp.bfloat16)
    flipped = jnp.concatenate(
        [
            jnp.concatenate([last[HD : 2 * HD, :].T, ones], axis=0),
            jnp.concatenate([last[3 * HD :, :].T, ones], axis=0),
        ],
        axis=1,
    )
    stats[...] = jnp.zeros_like(stats)
    for t in range(TILES):
        slot, first = tile_of(t)
        rows = query_rows(queries, slot, first)
        found = [
            masked_scores(
                spans, order, offset, last[2 * half * HD : (2 * half + 1) * HD, :],
                rows, t, half == 0, start,
            )
            for half in range(2)
        ]
        before = tops[t, 0:1, :]
        top = jnp.max(jnp.maximum(highest(found[0]), highest(found[1])), axis=0, keepdims=True)
        top = jnp.maximum(top, before)
        weights = [jnp.exp2((f - top) * FACTOR).astype(jnp.bfloat16) for f in found]
        summed = sums[t] * jnp.exp2((before - top) * FACTOR) + dot(
            flipped, jnp.concatenate(weights, axis=0), NN
        )
        total = summed[HD : HD + 1, :]
        normal = summed[:HD, :] * (1.0 / jnp.maximum(total, 1e-30))
        for j in range(TILE // HD):
            cut = slice(j * HD, (j + 1) * HD)
            out[first + j, slot * HD : (slot + 1) * HD, :] = normal[:, cut].astype(jnp.bfloat16)
            write_stats(stats, first + j, slot, top[:, cut], total[:, cut])
    out[:, FAR * HD :, :] = stats[...].astype(jnp.bfloat16)


def project_kernel(spans, parts, near, weight, out, kept, attn):
    order = head_order(spans)
    terms = parts[:, FAR * HD :, :].astype(jnp.float32)
    for s in range(FAR):
        level = [
            terms[i, 4 * s : 4 * s + 1] + terms[i, 4 * s + 1 : 4 * s + 2] + terms[i, 4 * s + 2 : 4 * s + 3]
            for i in range(BLOCKS)
        ]
        top = level[0]
        for i in range(1, BLOCKS):
            top = jnp.maximum(top, level[i])
        share = [jnp.exp2(v - top) for v in level]
        total = share[0]
        for i in range(1, BLOCKS):
            total = total + share[i]
        summed = jnp.zeros((HD, HD), jnp.float32)
        for i in range(BLOCKS):
            summed = summed + parts[i, s * HD : (s + 1) * HD, :].astype(jnp.float32) * share[i]
        attn[:, pl.ds(pl.multiple_of(order[s] * HD, HD), HD)] = (
            (summed * (1.0 / total)).T.astype(jnp.bfloat16)
        )
    for s in range(FAR, GROUP):
        attn[:, pl.ds(pl.multiple_of(order[s] * HD, HD), HD)] = near[s - FAR]
    rows = attn[...]
    mine = lax.axis_index("c")
    width = out.shape[2]
    for core, target in ((1 - mine, out), (mine, kept)):
        for f in range(out.shape[0]):
            at = pl.multiple_of((2 * f + core) * width, width)
            product = dot(rows, weight[:, pl.ds(at, width)], NN)
            target[f] = product.astype(target.dtype)


def add_kernel(kept, received, out):
    out[...] = (kept[...] + received[...].astype(jnp.float32)).astype(jnp.bfloat16)


def total_kernel(shares, out):
    total = shares[0].astype(jnp.float32)
    for i in range(1, shares.shape[0]):
        total = total + shares[i].astype(jnp.float32)
    out[...] = total.T.astype(jnp.bfloat16)


def call(kernel, outs, specs, scratch=(), vmem=24, flops=0, moved=0, exps=0):
    single = not isinstance(outs, list)
    return pl.pallas_call(
        kernel,
        out_shape=outs,
        in_specs=specs,
        out_specs=VMEM if single else [VMEM] * len(outs),
        scratch_shapes=list(scratch),
        compiler_params=pltpu.CompilerParams(vmem_limit_bytes=vmem * 2**20),
        cost_estimate=pl.CostEstimate(flops=flops, bytes_accessed=moved, transcendentals=exps),
    )


def per_device(queries, keys, values, cache_keys, cache_values, spans, out_weight):
    bf16, f32 = jnp.bfloat16, jnp.float32
    own, own_rows = call(
        prepare_kernel,
        [
            jax.ShapeDtypeStruct((4 * HD, HD), bf16),
            jax.ShapeDtypeStruct((GROUP * HD, HD), bf16),
        ],
        [ANY] * 6,
        [
            pltpu.VMEM((HD, GROUP * HD), bf16),
            pltpu.SMEM((GROUP,), jnp.int32),
            pltpu.SemaphoreType.DMA((6,)),
        ],
        vmem=60,
        moved=2**20,
    )(spans, queries, keys, values, cache_keys, cache_values)
    routes = [
        [
            (2 * i + c, (i + (1 if c == turn else -1)) % RING * 2 + c)
            for i in range(RING)
            for c in range(2)
        ]
        for turn in range(2)
    ]
    kv, one, two = [own], own, own
    for _ in range(RING // 2 - 1):
        one = lax.ppermute(one, ("k", "c"), routes[0])
        two = lax.ppermute(two, ("k", "c"), routes[1])
        kv += [one, two]
    last = lax.ppermute(one, ("k", "c"), routes[0])
    sent, kv[0], near_rows = call(
        hand_kernel,
        [
            jax.ShapeDtypeStruct((BLOCKS, 4 * HD, HD), bf16),
            jax.ShapeDtypeStruct((4 * HD, HD), bf16),
            jax.ShapeDtypeStruct((2 * HD, HD), bf16),
        ],
        [VMEM] * 4,
        moved=2**20,
    )(own_rows, own, kv[1], kv[2])
    grouped = lax.all_to_all(sent, ("e", "x"), 0, 0, tiled=True)
    near_blocks = 2 * (RING - 1)
    sums, tops, near = call(
        first_kernel,
        [
            jax.ShapeDtypeStruct((TILES, HD + STATS, TILE), f32),
            jax.ShapeDtypeStruct((TILES, 8, TILE), f32),
            jax.ShapeDtypeStruct((2, HD, HD), bf16),
        ],
        [SMEM] + [VMEM] * (RING + 1),
        [
            pltpu.VMEM((near_blocks * HD, HD), bf16),
            pltpu.VMEM((HD + STATS, near_blocks * HD), bf16),
            pltpu.VMEM((2, near_blocks * HD, TILE), f32),
        ],
        flops=4 * 2048 * 1792 * 128,
        moved=4 * 2**20,
        exps=2048 * 1792,
    )(spans, near_rows, grouped, *kv)
    partial = call(
        second_kernel,
        jax.ShapeDtypeStruct((BLOCKS, PIECE, HD), bf16),
        [SMEM] + [VMEM] * 4,
        [pltpu.VMEM((BLOCKS, STATS, HD), f32)],
        flops=4 * 2048 * 256 * 128,
        moved=4 * 2**20,
        exps=2048 * 256,
    )(spans, grouped, last, sums, tops)
    parts = lax.all_to_all(partial, ("e", "x"), 0, 0, tiled=True)
    width = out_weight.shape[1] // 8
    product, kept = call(
        project_kernel,
        [
            jax.ShapeDtypeStruct((4, HD, width), bf16),
            jax.ShapeDtypeStruct((4, HD, width), f32),
        ],
        [SMEM, VMEM, VMEM, VMEM],
        [pltpu.VMEM((HD, GROUP * HD), bf16)],
        flops=2 * 128 * 512 * 4096,
        moved=5 * 2**20,
    )(spans, parts, near, out_weight)
    received = lax.ppermute(product, "c", [(0, 1), (1, 0)])
    halves = call(
        add_kernel,
        jax.ShapeDtypeStruct((4, HD, width), bf16),
        [VMEM] * 2,
        moved=2 * 2**20,
    )(kept, received)
    shares = lax.all_to_all(halves, "y", 0, 0, tiled=True)
    return call(
        total_kernel,
        jax.ShapeDtypeStruct((width, HD), bf16),
        [VMEM],
        moved=2**20,
    )(shares)


def solution(mesh):
    fine = Mesh(mesh.devices.reshape(RING, 2, 4, 4, 2), ("k", "e", "x", "y", "c"))
    seq, head = ("k", "e", "x"), ("y", "c")
    placed = (P(seq, head),) * 5 + (P(head), P(head, None))
    return jax.shard_map(
        per_device, mesh=fine, in_specs=placed, out_specs=P(head, seq), check_vma=False
    )
```

```python
import math

import jax
import jax.numpy as jnp
from jax import lax
from jax.experimental import pallas as pl
from jax.experimental.pallas import tpu as pltpu
from jax.sharding import Mesh
from jax.sharding import PartitionSpec as P

HD = 128
GROUP = 4
FAR = 2
BLOCKS = 8
RING = 8
STATS = 16
PIECE = FAR * HD + STATS
MASKED = -1e30
FLOOR = -1e29
FACTOR = math.log2(math.e) / math.sqrt(HD)
TILE = 2 * HD
TILES = 2 * BLOCKS * HD // TILE
CACHE = 2 * RING * BLOCKS // 2 * HD
VMEM = pl.BlockSpec(memory_space=pltpu.VMEM)
SMEM = pl.BlockSpec(memory_space=pltpu.SMEM)
ANY = pl.BlockSpec(memory_space=pl.ANY)
NT = (((1,), (1,)), ((), ()))
NN = (((1,), (0,)), ((), ()))


def dot(a, b, dims):
    return lax.dot_general(a, b, dims, preferred_element_type=jnp.float32)


def head_order(spans):
    far = [(spans[h] > 4 * HD).astype(jnp.int32) for h in range(GROUP)]
    order = [jnp.int32(0)] * GROUP
    ahead = jnp.int32(0)
    for h in range(GROUP):
        rank = jnp.where(far[h] == 1, ahead, 2 + h - ahead)
        ahead = ahead + far[h]
        order = [jnp.where(rank == s, h, order[s]) for s in range(GROUP)]
    return order


def prepare_kernel(
    spans, queries, keys, values, cache_keys, cache_values, own, own_rows, handed, heads, kinds, sems
):
    copies = [
        pltpu.make_async_copy(spans, kinds, sems.at[0]),
        pltpu.make_async_copy(queries, heads, sems.at[1]),
    ]
    for i, source in enumerate([cache_keys, cache_values, keys, values]):
        copies.append(
            pltpu.make_async_copy(source, own.at[i * HD : (i + 1) * HD, :], sems.at[2 + i])
        )
    for copy in copies:
        copy.start()
    for copy in copies:
        copy.wait()
    k, e, _ = position()
    ends = (k == RING - 1) & (e == 1)
    handed[...] = jnp.where(ends, own[: 2 * HD, :], own[2 * HD :, :])
    order = head_order(kinds)
    for s in range(GROUP):
        rows = heads[:, pl.ds(pl.multiple_of(order[s] * HD, HD), HD)]
        own_rows[s * HD : (s + 1) * HD, :] = rows


def spread_kernel(own_rows, other_rows, own, prior, after, sent, held, near_rows):
    del after
    first = lax.axis_index("e") == 0
    mine, other = own_rows[: FAR * HD, :], other_rows[: FAR * HD, :]
    lower = jnp.where(first, mine, other)
    upper = jnp.where(first, other, mine)
    for j in range(4):
        sent[j, : 2 * HD, :] = lower
        sent[j, 2 * HD : 4 * HD, :] = upper
        sent[j, 4 * HD : 6 * HD, :] = own[2 * HD :, :]
        sent[j, 6 * HD :, :] = prior[...]
    held[...] = own[...]
    near_rows[...] = own_rows[FAR * HD :, :]


def query_rows(gathered, slot, first):
    at = first // 4 * 2 * HD + slot * HD
    return gathered[first % 4 : first % 4 + TILE // HD, at : at + HD, :].reshape(TILE, HD)


def position():
    return lax.axis_index("k"), lax.axis_index("e"), lax.axis_index("x")


def place(distance):
    k, e, x = position()
    return ((lax.rem(k + distance + RING, RING) * 2 + e) * 4 + x) * HD


def sources():
    first = jnp.where(lax.axis_index("c") == 0, -1, 1)
    return [0 * first, first, -first, 2 * first, -2 * first, 3 * first, -3 * first, 4 * first]


def offsets():
    token = lax.broadcasted_iota(jnp.int32, (HD, TILE), 1)
    return lax.rem(token, HD), token - lax.broadcasted_iota(jnp.int32, (HD, TILE), 0)


def tile_of(t):
    per = TILE // HD
    return t // (BLOCKS // per), t % (BLOCKS // per) * per


def masked_scores(spans, order, offset, key_rows, rows, t, cached, start):
    slot, first = tile_of(t)
    begin = CACHE + lax.axis_index("k") * (BLOCKS * HD) + first * HD
    found = dot(key_rows, rows, NT)
    if cached:
        allowed = offset < spans[order[slot]] - begin + start
    else:
        allowed = offset >= start + CACHE - begin
    return jnp.where(allowed, found, MASKED)


def highest(found):
    return jnp.max(found.reshape(HD // 8, 8, found.shape[1]), axis=0)


def near_heads(spans, order, rows, own, gathered, out):
    x = lax.axis_index("x")
    column, _ = offsets()
    behind = column - lax.broadcasted_iota(jnp.int32, (HD, TILE), 0)
    span = jnp.where(
        lax.broadcasted_iota(jnp.int32, (HD, TILE), 1) < HD, spans[order[2]], spans[order[3]]
    )
    found, values = [], []
    for j in range(5):
        if j < 4:
            distance = jnp.where(j < x, x - j, x - j + 4) * HD
            block = jnp.where(j < x, gathered[j, 4 * HD : 6 * HD, :], gathered[j, 6 * HD :, :])
            key_rows, value_rows = block[:HD, :], block[HD:, :]
        else:
            distance = 0
            key_rows, value_rows = own[2 * HD : 3 * HD, :], own[3 * HD :, :]
        far = behind + distance
        found.append(
            jnp.where((far >= 0) & (far < span), dot(key_rows, rows[...], NT), MASKED)
        )
        values.append(value_rows)
    top = highest(found[0])
    for j in range(1, 5):
        top = jnp.maximum(top, highest(found[j]))
    top = jnp.max(top, axis=0, keepdims=True)
    weights = jnp.concatenate(
        [jnp.exp2((f - top) * FACTOR).astype(jnp.bfloat16) for f in found], axis=0
    )
    flipped = jnp.concatenate([v.T for v in values], axis=1)
    flipped = jnp.concatenate([flipped, jnp.ones((STATS, 5 * HD), jnp.bfloat16)], axis=0)
    summed = dot(flipped, weights, NN)
    normal = summed[:HD, :] * (1.0 / summed[HD : HD + 1, :])
    for s in range(2):
        out[s] = normal[:, s * HD : (s + 1) * HD].T.astype(jnp.bfloat16)


def first_kernel(spans, near_rows, queries, *refs):
    kv = refs[: RING - 1]
    sums, tops, near, keys, flipped, scores = refs[RING - 1 :]
    order = head_order(spans)
    distances = sources()
    blocks = []
    for i in range(RING - 1):
        for half in range(2):
            n = len(blocks)
            blocks.append((half == 0, place(distances[i])))
            keys[n * HD : (n + 1) * HD, :] = kv[i][2 * half * HD : (2 * half + 1) * HD, :]
            flipped[0:HD, n * HD : (n + 1) * HD] = kv[i][
                (2 * half + 1) * HD : (2 * half + 2) * HD, :
            ].T
    width = len(blocks) * HD
    flipped[HD:, :] = jnp.ones((STATS, width), jnp.bfloat16)
    _, offset = offsets()

    def score(t):
        slot, first = tile_of(t)
        rows = query_rows(queries, slot, first)
        top = jnp.full((8, TILE), FLOOR, jnp.float32)
        for n, (cached, start) in enumerate(blocks):
            found = masked_scores(
                spans, order, offset, keys[n * HD : (n + 1) * HD, :], rows, t, cached, start
            )
            scores[t % 2, n * HD : (n + 1) * HD, :] = found
            top = jnp.maximum(top, highest(found))
        return jnp.max(top, axis=0, keepdims=True)

    def finish(t, top):
        weights = jnp.concatenate(
            [
                jnp.exp2((scores[t % 2, n * HD : (n + 1) * HD, :] - top) * FACTOR).astype(
                    jnp.bfloat16
                )
                for n in range(len(blocks))
            ],
            axis=0,
        )
        sums[t] = dot(flipped[...], weights, NN)
        tops[t] = jnp.broadcast_to(top, (8, TILE))

    near_heads(spans, order, near_rows, kv[0], queries, near)
    top = score(0)
    for t in range(TILES):
        later = score(t + 1) if t + 1 < TILES else None
        finish(t, top)
        top = later


def write_stats(stats, block, slot, top, total):
    level = jnp.where(total > 0.0, top * FACTOR + jnp.log2(total), MASKED)
    for i in range(3):
        term = level.astype(jnp.bfloat16).astype(jnp.float32)
        stats[block, slot * 4 + i : slot * 4 + i + 1, :] = term
        level = level - term


def second_kernel(spans, queries, last, sums, tops, out, stats):
    order = head_order(spans)
    start = place(sources()[-1])
    _, offset = offsets()
    ones = jnp.ones((STATS, HD), jnp.bfloat16)
    flipped = jnp.concatenate(
        [
            jnp.concatenate([last[HD : 2 * HD, :].T, ones], axis=0),
            jnp.concatenate([last[3 * HD :, :].T, ones], axis=0),
        ],
        axis=1,
    )
    stats[...] = jnp.zeros_like(stats)
    for t in range(TILES):
        slot, first = tile_of(t)
        rows = query_rows(queries, slot, first)
        found = [
            masked_scores(
                spans, order, offset, last[2 * half * HD : (2 * half + 1) * HD, :],
                rows, t, half == 0, start,
            )
            for half in range(2)
        ]
        before = tops[t, 0:1, :]
        top = jnp.max(jnp.maximum(highest(found[0]), highest(found[1])), axis=0, keepdims=True)
        top = jnp.maximum(top, before)
        weights = [jnp.exp2((f - top) * FACTOR).astype(jnp.bfloat16) for f in found]
        summed = sums[t] * jnp.exp2((before - top) * FACTOR) + dot(
            flipped, jnp.concatenate(weights, axis=0), NN
        )
        total = summed[HD : HD + 1, :]
        normal = summed[:HD, :] * (1.0 / jnp.maximum(total, 1e-30))
        for j in range(TILE // HD):
            cut = slice(j * HD, (j + 1) * HD)
            out[first + j, slot * HD : (slot + 1) * HD, :] = normal[:, cut].astype(jnp.bfloat16)
            write_stats(stats, first + j, slot, top[:, cut], total[:, cut])
    out[:, FAR * HD :, :] = stats[...].astype(jnp.bfloat16)


def project_kernel(spans, parts, near, weight, out, kept, attn):
    order = head_order(spans)
    terms = parts[:, FAR * HD :, :].astype(jnp.float32)
    for s in range(FAR):
        level = [
            terms[i, 4 * s : 4 * s + 1] + terms[i, 4 * s + 1 : 4 * s + 2] + terms[i, 4 * s + 2 : 4 * s + 3]
            for i in range(BLOCKS)
        ]
        top = level[0]
        for i in range(1, BLOCKS):
            top = jnp.maximum(top, level[i])
        share = [jnp.exp2(v - top) for v in level]
        total = share[0]
        for i in range(1, BLOCKS):
            total = total + share[i]
        summed = jnp.zeros((HD, HD), jnp.float32)
        for i in range(BLOCKS):
            summed = summed + parts[i, s * HD : (s + 1) * HD, :].astype(jnp.float32) * share[i]
        attn[:, pl.ds(pl.multiple_of(order[s] * HD, HD), HD)] = (
            (summed * (1.0 / total)).T.astype(jnp.bfloat16)
        )
    for s in range(FAR, GROUP):
        attn[:, pl.ds(pl.multiple_of(order[s] * HD, HD), HD)] = near[s - FAR]
    rows = attn[...]
    mine = lax.axis_index("c")
    width = out.shape[2]
    for core, target in ((1 - mine, out), (mine, kept)):
        for f in range(out.shape[0]):
            at = pl.multiple_of((2 * f + core) * width, width)
            product = dot(rows, weight[:, pl.ds(at, width)], NN)
            target[f] = product.astype(target.dtype)


def add_kernel(kept, received, out):
    out[...] = (kept[...] + received[...].astype(jnp.float32)).astype(jnp.bfloat16)


def total_kernel(shares, out):
    total = shares[0].astype(jnp.float32)
    for i in range(1, shares.shape[0]):
        total = total + shares[i].astype(jnp.float32)
    out[...] = total.T.astype(jnp.bfloat16)


def call(kernel, outs, specs, scratch=(), vmem=24, flops=0, moved=0, exps=0):
    single = not isinstance(outs, list)
    return pl.pallas_call(
        kernel,
        out_shape=outs,
        in_specs=specs,
        out_specs=VMEM if single else [VMEM] * len(outs),
        scratch_shapes=list(scratch),
        compiler_params=pltpu.CompilerParams(vmem_limit_bytes=vmem * 2**20),
        cost_estimate=pl.CostEstimate(flops=flops, bytes_accessed=moved, transcendentals=exps),
    )


def per_device(queries, keys, values, cache_keys, cache_values, spans, out_weight):
    bf16, f32 = jnp.bfloat16, jnp.float32
    own, own_rows, handed = call(
        prepare_kernel,
        [
            jax.ShapeDtypeStruct((4 * HD, HD), bf16),
            jax.ShapeDtypeStruct((GROUP * HD, HD), bf16),
            jax.ShapeDtypeStruct((2 * HD, HD), bf16),
        ],
        [ANY] * 6,
        [
            pltpu.VMEM((HD, GROUP * HD), bf16),
            pltpu.SMEM((GROUP,), jnp.int32),
            pltpu.SemaphoreType.DMA((6,)),
        ],
        vmem=60,
        moved=2**20,
    )(spans, queries, keys, values, cache_keys, cache_values)
    other_rows = lax.ppermute(own_rows, "e", [(0, 1), (1, 0)])
    prior = lax.ppermute(
        handed, ("k", "e"), [(i, (i + 1) % (2 * RING)) for i in range(2 * RING)]
    )
    routes = [
        [
            (2 * i + c, (i + (1 if c == turn else -1)) % RING * 2 + c)
            for i in range(RING)
            for c in range(2)
        ]
        for turn in range(2)
    ]
    kv, one = [own], own
    two, other_rows, prior = lax.optimization_barrier((own, other_rows, prior))
    for _ in range(RING // 2 - 1):
        one = lax.ppermute(one, ("k", "c"), routes[0])
        two = lax.ppermute(two, ("k", "c"), routes[1])
        kv += [one, two]
    last = lax.ppermute(one, ("k", "c"), routes[0])
    sent, kv[0], near_rows = call(
        spread_kernel,
        [
            jax.ShapeDtypeStruct((4, 8 * HD, HD), bf16),
            jax.ShapeDtypeStruct((4 * HD, HD), bf16),
            jax.ShapeDtypeStruct((2 * HD, HD), bf16),
        ],
        [VMEM] * 4 + [ANY],
        moved=2**20,
    )(own_rows, other_rows, own, prior, kv[1])
    grouped = lax.all_to_all(sent, "x", 0, 0, tiled=True)
    near_blocks = 2 * (RING - 1)
    sums, tops, near = call(
        first_kernel,
        [
            jax.ShapeDtypeStruct((TILES, HD + STATS, TILE), f32),
            jax.ShapeDtypeStruct((TILES, 8, TILE), f32),
            jax.ShapeDtypeStruct((2, HD, HD), bf16),
        ],
        [SMEM] + [VMEM] * (RING + 1),
        [
            pltpu.VMEM((near_blocks * HD, HD), bf16),
            pltpu.VMEM((HD + STATS, near_blocks * HD), bf16),
            pltpu.VMEM((2, near_blocks * HD, TILE), f32),
        ],
        flops=4 * 2048 * 1792 * 128,
        moved=4 * 2**20,
        exps=2048 * 1792,
    )(spans, near_rows, grouped, *kv)
    partial = call(
        second_kernel,
        jax.ShapeDtypeStruct((BLOCKS, PIECE, HD), bf16),
        [SMEM] + [VMEM] * 4,
        [pltpu.VMEM((BLOCKS, STATS, HD), f32)],
        flops=4 * 2048 * 256 * 128,
        moved=4 * 2**20,
        exps=2048 * 256,
    )(spans, grouped, last, sums, tops)
    parts = lax.all_to_all(partial, ("e", "x"), 0, 0, tiled=True)
    width = out_weight.shape[1] // 8
    product, kept = call(
        project_kernel,
        [
            jax.ShapeDtypeStruct((4, HD, width), bf16),
            jax.ShapeDtypeStruct((4, HD, width), f32),
        ],
        [SMEM, VMEM, VMEM, VMEM],
        [pltpu.VMEM((HD, GROUP * HD), bf16)],
        flops=2 * 128 * 512 * 4096,
        moved=5 * 2**20,
    )(spans, parts, near, out_weight)
    received = lax.ppermute(product, "c", [(0, 1), (1, 0)])
    halves = call(
        add_kernel,
        jax.ShapeDtypeStruct((4, HD, width), bf16),
        [VMEM] * 2,
        moved=2 * 2**20,
    )(kept, received)
    shares = lax.all_to_all(halves, "y", 0, 0, tiled=True)
    return call(
        total_kernel,
        jax.ShapeDtypeStruct((width, HD), bf16),
        [VMEM],
        moved=2**20,
    )(shares)


def solution(mesh):
    fine = Mesh(mesh.devices.reshape(RING, 2, 4, 4, 2), ("k", "e", "x", "y", "c"))
    seq, head = ("k", "e", "x"), ("y", "c")
    placed = (P(seq, head),) * 5 + (P(head), P(head, None))
    return jax.shard_map(
        per_device, mesh=fine, in_specs=placed, out_specs=P(head, seq), check_vma=False
    )
```

```python
import math

import jax
import jax.numpy as jnp
from jax import lax
from jax.experimental import pallas as pl
from jax.experimental.pallas import tpu as pltpu
from jax.sharding import Mesh
from jax.sharding import PartitionSpec as P

HD = 128
GROUP = 4
FAR = 2
BLOCKS = 8
RING = 8
STATS = 16
PIECE = FAR * HD + STATS
MASKED = -1e30
FLOOR = -1e29
FACTOR = math.log2(math.e) / math.sqrt(HD)
TILE = 2 * HD
TILES = 2 * BLOCKS * HD // TILE
CACHE = 2 * RING * BLOCKS // 2 * HD
VMEM = pl.BlockSpec(memory_space=pltpu.VMEM)
SMEM = pl.BlockSpec(memory_space=pltpu.SMEM)
ANY = pl.BlockSpec(memory_space=pl.ANY)
NT = (((1,), (1,)), ((), ()))
NN = (((1,), (0,)), ((), ()))


def dot(a, b, dims):
    return lax.dot_general(a, b, dims, preferred_element_type=jnp.float32)


def head_order(spans):
    far = [(spans[h] > 4 * HD).astype(jnp.int32) for h in range(GROUP)]
    order = [jnp.int32(0)] * GROUP
    ahead = jnp.int32(0)
    for h in range(GROUP):
        rank = jnp.where(far[h] == 1, ahead, 2 + h - ahead)
        ahead = ahead + far[h]
        order = [jnp.where(rank == s, h, order[s]) for s in range(GROUP)]
    return order


def prepare_kernel(
    spans, queries, keys, values, cache_keys, cache_values, own, own_rows, handed, heads, kinds, sems
):
    copies = [
        pltpu.make_async_copy(spans, kinds, sems.at[0]),
        pltpu.make_async_copy(queries, heads, sems.at[1]),
    ]
    for i, source in enumerate([cache_keys, cache_values, keys, values]):
        copies.append(
            pltpu.make_async_copy(source, own.at[i * HD : (i + 1) * HD, :], sems.at[2 + i])
        )
    for copy in copies:
        copy.start()
    for copy in copies:
        copy.wait()
    k, e, _ = position()
    ends = (k == RING - 1) & (e == 1)
    handed[...] = jnp.where(ends, own[: 2 * HD, :], own[2 * HD :, :])
    order = head_order(kinds)
    for s in range(GROUP):
        rows = heads[:, pl.ds(pl.multiple_of(order[s] * HD, HD), HD)]
        own_rows[s * HD : (s + 1) * HD, :] = rows


def spread_kernel(own_rows, other_rows, own, prior, after, after_too, sent, held, near_rows):
    del after, after_too
    first = lax.axis_index("e") == 0
    mine, other = own_rows[: FAR * HD, :], other_rows[: FAR * HD, :]
    lower = jnp.where(first, mine, other)
    upper = jnp.where(first, other, mine)
    for j in range(4):
        sent[j, : 2 * HD, :] = lower
        sent[j, 2 * HD : 4 * HD, :] = upper
        sent[j, 4 * HD : 6 * HD, :] = own[2 * HD :, :]
        sent[j, 6 * HD :, :] = prior[...]
    held[...] = own[...]
    near_rows[...] = own_rows[FAR * HD :, :]


def query_rows(gathered, slot, first):
    at = first // 4 * 2 * HD + slot * HD
    return gathered[first % 4 : first % 4 + TILE // HD, at : at + HD, :].reshape(TILE, HD)


def position():
    return lax.axis_index("k"), lax.axis_index("e"), lax.axis_index("x")


def place(distance):
    k, e, x = position()
    return ((lax.rem(k + distance + RING, RING) * 2 + e) * 4 + x) * HD


def sources():
    first = jnp.where(lax.axis_index("c") == 0, -1, 1)
    return [0 * first, first, -first, 2 * first, -2 * first, 3 * first, -3 * first, 4 * first]


def offsets():
    token = lax.broadcasted_iota(jnp.int32, (HD, TILE), 1)
    return lax.rem(token, HD), token - lax.broadcasted_iota(jnp.int32, (HD, TILE), 0)


def tile_of(t):
    per = TILE // HD
    return t // (BLOCKS // per), t % (BLOCKS // per) * per


def masked_scores(spans, order, offset, key_rows, rows, t, cached, start):
    slot, first = tile_of(t)
    begin = CACHE + lax.axis_index("k") * (BLOCKS * HD) + first * HD
    found = dot(key_rows, rows, NT)
    if cached:
        allowed = offset < spans[order[slot]] - begin + start
    else:
        allowed = offset >= start + CACHE - begin
    return jnp.where(allowed, found, MASKED)


def highest(found):
    return jnp.max(found.reshape(HD // 8, 8, found.shape[1]), axis=0)


def near_heads(spans, order, rows, own, gathered, out):
    x = lax.axis_index("x")
    column, _ = offsets()
    behind = column - lax.broadcasted_iota(jnp.int32, (HD, TILE), 0)
    span = jnp.where(
        lax.broadcasted_iota(jnp.int32, (HD, TILE), 1) < HD, spans[order[2]], spans[order[3]]
    )
    found, values = [], []
    for j in range(5):
        if j < 4:
            distance = jnp.where(j < x, x - j, x - j + 4) * HD
            block = jnp.where(j < x, gathered[j, 4 * HD : 6 * HD, :], gathered[j, 6 * HD :, :])
            key_rows, value_rows = block[:HD, :], block[HD:, :]
        else:
            distance = 0
            key_rows, value_rows = own[2 * HD : 3 * HD, :], own[3 * HD :, :]
        far = behind + distance
        found.append(
            jnp.where((far >= 0) & (far < span), dot(key_rows, rows[...], NT), MASKED)
        )
        values.append(value_rows)
    top = highest(found[0])
    for j in range(1, 5):
        top = jnp.maximum(top, highest(found[j]))
    top = jnp.max(top, axis=0, keepdims=True)
    weights = jnp.concatenate(
        [jnp.exp2((f - top) * FACTOR).astype(jnp.bfloat16) for f in found], axis=0
    )
    flipped = jnp.concatenate([v.T for v in values], axis=1)
    flipped = jnp.concatenate([flipped, jnp.ones((STATS, 5 * HD), jnp.bfloat16)], axis=0)
    summed = dot(flipped, weights, NN)
    normal = summed[:HD, :] * (1.0 / summed[HD : HD + 1, :])
    for s in range(2):
        out[s] = normal[:, s * HD : (s + 1) * HD].T.astype(jnp.bfloat16)


def first_kernel(spans, near_rows, queries, *refs):
    kv = refs[: RING - 1]
    sums, tops, near, keys, flipped, scores = refs[RING - 1 :]
    order = head_order(spans)
    distances = sources()
    blocks = []
    for i in range(RING - 1):
        for half in range(2):
            n = len(blocks)
            blocks.append((half == 0, place(distances[i])))
            keys[n * HD : (n + 1) * HD, :] = kv[i][2 * half * HD : (2 * half + 1) * HD, :]
            flipped[0:HD, n * HD : (n + 1) * HD] = kv[i][
                (2 * half + 1) * HD : (2 * half + 2) * HD, :
            ].T
    width = len(blocks) * HD
    flipped[HD:, :] = jnp.ones((STATS, width), jnp.bfloat16)
    _, offset = offsets()

    def score(t):
        slot, first = tile_of(t)
        rows = query_rows(queries, slot, first)
        top = jnp.full((8, TILE), FLOOR, jnp.float32)
        for n, (cached, start) in enumerate(blocks):
            found = masked_scores(
                spans, order, offset, keys[n * HD : (n + 1) * HD, :], rows, t, cached, start
            )
            scores[t % 2, n * HD : (n + 1) * HD, :] = found
            top = jnp.maximum(top, highest(found))
        return jnp.max(top, axis=0, keepdims=True)

    def finish(t, top):
        weights = jnp.concatenate(
            [
                jnp.exp2((scores[t % 2, n * HD : (n + 1) * HD, :] - top) * FACTOR).astype(
                    jnp.bfloat16
                )
                for n in range(len(blocks))
            ],
            axis=0,
        )
        sums[t] = dot(flipped[...], weights, NN)
        tops[t] = jnp.broadcast_to(top, (8, TILE))

    near_heads(spans, order, near_rows, kv[0], queries, near)
    top = score(0)
    for t in range(TILES):
        later = score(t + 1) if t + 1 < TILES else None
        finish(t, top)
        top = later


def write_stats(stats, block, slot, top, total):
    level = jnp.where(total > 0.0, top * FACTOR + jnp.log2(total), MASKED)
    for i in range(3):
        term = level.astype(jnp.bfloat16).astype(jnp.float32)
        stats[block, slot * 4 + i : slot * 4 + i + 1, :] = term
        level = level - term


def second_kernel(spans, queries, last, sums, tops, out, stats):
    order = head_order(spans)
    start = place(sources()[-1])
    _, offset = offsets()
    ones = jnp.ones((STATS, HD), jnp.bfloat16)
    flipped = jnp.concatenate(
        [
            jnp.concatenate([last[HD : 2 * HD, :].T, ones], axis=0),
            jnp.concatenate([last[3 * HD :, :].T, ones], axis=0),
        ],
        axis=1,
    )
    stats[...] = jnp.zeros_like(stats)
    for t in range(TILES):
        slot, first = tile_of(t)
        rows = query_rows(queries, slot, first)
        found = [
            masked_scores(
                spans, order, offset, last[2 * half * HD : (2 * half + 1) * HD, :],
                rows, t, half == 0, start,
            )
            for half in range(2)
        ]
        before = tops[t, 0:1, :]
        top = jnp.max(jnp.maximum(highest(found[0]), highest(found[1])), axis=0, keepdims=True)
        top = jnp.maximum(top, before)
        weights = [jnp.exp2((f - top) * FACTOR).astype(jnp.bfloat16) for f in found]
        summed = sums[t] * jnp.exp2((before - top) * FACTOR) + dot(
            flipped, jnp.concatenate(weights, axis=0), NN
        )
        total = summed[HD : HD + 1, :]
        normal = summed[:HD, :] * (1.0 / jnp.maximum(total, 1e-30))
        for j in range(TILE // HD):
            cut = slice(j * HD, (j + 1) * HD)
            out[first + j, slot * HD : (slot + 1) * HD, :] = normal[:, cut].astype(jnp.bfloat16)
            write_stats(stats, first + j, slot, top[:, cut], total[:, cut])
    out[:, FAR * HD :, :] = stats[...].astype(jnp.bfloat16)


def project_kernel(spans, parts, near, weight, out, kept, attn):
    order = head_order(spans)
    terms = parts[:, FAR * HD :, :].astype(jnp.float32)
    for s in range(FAR):
        level = [
            terms[i, 4 * s : 4 * s + 1] + terms[i, 4 * s + 1 : 4 * s + 2] + terms[i, 4 * s + 2 : 4 * s + 3]
            for i in range(BLOCKS)
        ]
        top = level[0]
        for i in range(1, BLOCKS):
            top = jnp.maximum(top, level[i])
        share = [jnp.exp2(v - top) for v in level]
        total = share[0]
        for i in range(1, BLOCKS):
            total = total + share[i]
        summed = jnp.zeros((HD, HD), jnp.float32)
        for i in range(BLOCKS):
            summed = summed + parts[i, s * HD : (s + 1) * HD, :].astype(jnp.float32) * share[i]
        attn[:, pl.ds(pl.multiple_of(order[s] * HD, HD), HD)] = (
            (summed * (1.0 / total)).T.astype(jnp.bfloat16)
        )
    for s in range(FAR, GROUP):
        attn[:, pl.ds(pl.multiple_of(order[s] * HD, HD), HD)] = near[s - FAR]
    rows = attn[...]
    mine = lax.axis_index("c")
    width = out.shape[2]
    for core, target in ((1 - mine, out), (mine, kept)):
        for f in range(out.shape[0]):
            at = pl.multiple_of((2 * f + core) * width, width)
            product = dot(rows, weight[:, pl.ds(at, width)], NN)
            target[f] = product.astype(target.dtype)


def add_kernel(kept, received, out):
    out[...] = (kept[...] + received[...].astype(jnp.float32)).astype(jnp.bfloat16)


def total_kernel(shares, out):
    total = shares[0].astype(jnp.float32)
    for i in range(1, shares.shape[0]):
        total = total + shares[i].astype(jnp.float32)
    out[...] = total.T.astype(jnp.bfloat16)


def call(kernel, outs, specs, scratch=(), vmem=24, flops=0, moved=0, exps=0):
    single = not isinstance(outs, list)
    return pl.pallas_call(
        kernel,
        out_shape=outs,
        in_specs=specs,
        out_specs=VMEM if single else [VMEM] * len(outs),
        scratch_shapes=list(scratch),
        compiler_params=pltpu.CompilerParams(vmem_limit_bytes=vmem * 2**20),
        cost_estimate=pl.CostEstimate(flops=flops, bytes_accessed=moved, transcendentals=exps),
    )


def per_device(queries, keys, values, cache_keys, cache_values, spans, out_weight):
    bf16, f32 = jnp.bfloat16, jnp.float32
    own, own_rows, handed = call(
        prepare_kernel,
        [
            jax.ShapeDtypeStruct((4 * HD, HD), bf16),
            jax.ShapeDtypeStruct((GROUP * HD, HD), bf16),
            jax.ShapeDtypeStruct((2 * HD, HD), bf16),
        ],
        [ANY] * 6,
        [
            pltpu.VMEM((HD, GROUP * HD), bf16),
            pltpu.SMEM((GROUP,), jnp.int32),
            pltpu.SemaphoreType.DMA((6,)),
        ],
        vmem=60,
        moved=2**20,
    )(spans, queries, keys, values, cache_keys, cache_values)
    other_rows = lax.ppermute(own_rows, "e", [(0, 1), (1, 0)])
    prior = lax.ppermute(
        handed, ("k", "e"), [(i, (i + 1) % (2 * RING)) for i in range(2 * RING)]
    )
    routes = [
        [
            (2 * i + c, (i + (1 if c == turn else -1)) % RING * 2 + c)
            for i in range(RING)
            for c in range(2)
        ]
        for turn in range(2)
    ]
    kv, one, two = [own], own, own
    for step in range(RING // 2 - 1):
        one = lax.ppermute(one, ("k", "c"), routes[0])
        two = lax.ppermute(two, ("k", "c"), routes[1])
        kv += [one, two]
        if step == 0:
            one, two, other_rows, prior = lax.optimization_barrier((one, two, other_rows, prior))
    last = lax.ppermute(one, ("k", "c"), routes[0])
    sent, kv[0], near_rows = call(
        spread_kernel,
        [
            jax.ShapeDtypeStruct((4, 8 * HD, HD), bf16),
            jax.ShapeDtypeStruct((4 * HD, HD), bf16),
            jax.ShapeDtypeStruct((2 * HD, HD), bf16),
        ],
        [VMEM] * 4 + [ANY] * 2,
        moved=2**20,
    )(own_rows, other_rows, own, prior, kv[1], kv[2])
    grouped = lax.all_to_all(sent, "x", 0, 0, tiled=True)
    near_blocks = 2 * (RING - 1)
    sums, tops, near = call(
        first_kernel,
        [
            jax.ShapeDtypeStruct((TILES, HD + STATS, TILE), f32),
            jax.ShapeDtypeStruct((TILES, 8, TILE), f32),
            jax.ShapeDtypeStruct((2, HD, HD), bf16),
        ],
        [SMEM] + [VMEM] * (RING + 1),
        [
            pltpu.VMEM((near_blocks * HD, HD), bf16),
            pltpu.VMEM((HD + STATS, near_blocks * HD), bf16),
            pltpu.VMEM((2, near_blocks * HD, TILE), f32),
        ],
        flops=4 * 2048 * 1792 * 128,
        moved=4 * 2**20,
        exps=2048 * 1792,
    )(spans, near_rows, grouped, *kv)
    partial = call(
        second_kernel,
        jax.ShapeDtypeStruct((BLOCKS, PIECE, HD), bf16),
        [SMEM] + [VMEM] * 4,
        [pltpu.VMEM((BLOCKS, STATS, HD), f32)],
        flops=4 * 2048 * 256 * 128,
        moved=4 * 2**20,
        exps=2048 * 256,
    )(spans, grouped, last, sums, tops)
    parts = lax.all_to_all(partial, ("e", "x"), 0, 0, tiled=True)
    width = out_weight.shape[1] // 8
    product, kept = call(
        project_kernel,
        [
            jax.ShapeDtypeStruct((4, HD, width), bf16),
            jax.ShapeDtypeStruct((4, HD, width), f32),
        ],
        [SMEM, VMEM, VMEM, VMEM],
        [pltpu.VMEM((HD, GROUP * HD), bf16)],
        flops=2 * 128 * 512 * 4096,
        moved=5 * 2**20,
    )(spans, parts, near, out_weight)
    received = lax.ppermute(product, "c", [(0, 1), (1, 0)])
    halves = call(
        add_kernel,
        jax.ShapeDtypeStruct((4, HD, width), bf16),
        [VMEM] * 2,
        moved=2 * 2**20,
    )(kept, received)
    shares = lax.all_to_all(halves, "y", 0, 0, tiled=True)
    return call(
        total_kernel,
        jax.ShapeDtypeStruct((width, HD), bf16),
        [VMEM],
        moved=2**20,
    )(shares)


def solution(mesh):
    fine = Mesh(mesh.devices.reshape(RING, 2, 4, 4, 2), ("k", "e", "x", "y", "c"))
    seq, head = ("k", "e", "x"), ("y", "c")
    placed = (P(seq, head),) * 5 + (P(head), P(head, None))
    return jax.shard_map(
        per_device, mesh=fine, in_specs=placed, out_specs=P(head, seq), check_vma=False
    )
```

```python
import math

import jax
import jax.numpy as jnp
from jax import lax
from jax.experimental import pallas as pl
from jax.experimental.pallas import tpu as pltpu
from jax.sharding import Mesh
from jax.sharding import PartitionSpec as P

HD = 128
GROUP = 4
FAR = 2
BLOCKS = 8
RING = 8
STATS = 16
PIECE = FAR * HD + STATS
MASKED = -1e30
FLOOR = -1e29
FACTOR = math.log2(math.e) / math.sqrt(HD)
TILE = 2 * HD
TILES = 2 * BLOCKS * HD // TILE
CACHE = 2 * RING * BLOCKS // 2 * HD
VMEM = pl.BlockSpec(memory_space=pltpu.VMEM)
SMEM = pl.BlockSpec(memory_space=pltpu.SMEM)
ANY = pl.BlockSpec(memory_space=pl.ANY)
NT = (((1,), (1,)), ((), ()))
NN = (((1,), (0,)), ((), ()))


def dot(a, b, dims):
    return lax.dot_general(a, b, dims, preferred_element_type=jnp.float32)


def head_order(spans):
    far = [(spans[h] > 4 * HD).astype(jnp.int32) for h in range(GROUP)]
    order = [jnp.int32(0)] * GROUP
    ahead = jnp.int32(0)
    for h in range(GROUP):
        rank = jnp.where(far[h] == 1, ahead, 2 + h - ahead)
        ahead = ahead + far[h]
        order = [jnp.where(rank == s, h, order[s]) for s in range(GROUP)]
    return order


def prepare_kernel(
    spans, queries, keys, values, cache_keys, cache_values, own, own_rows, handed, joint, heads, kinds, sems
):
    copies = [
        pltpu.make_async_copy(spans, kinds, sems.at[0]),
        pltpu.make_async_copy(queries, heads, sems.at[1]),
    ]
    for i, source in enumerate([cache_keys, cache_values, keys, values]):
        copies.append(
            pltpu.make_async_copy(source, own.at[i * HD : (i + 1) * HD, :], sems.at[2 + i])
        )
    for copy in copies:
        copy.start()
    for copy in copies:
        copy.wait()
    k, e, _ = position()
    ends = (k == RING - 1) & (e == 1)
    handed[...] = jnp.where(ends, own[: 2 * HD, :], own[2 * HD :, :])
    order = head_order(kinds)
    for s in range(GROUP):
        rows = heads[:, pl.ds(pl.multiple_of(order[s] * HD, HD), HD)]
        own_rows[s * HD : (s + 1) * HD, :] = rows
        joint[(GROUP + s) * HD : (GROUP + s + 1) * HD, :] = rows
    joint[: GROUP * HD, :] = own[...]


def spread_kernel(joint, other_rows, prior, after, after_too, sent, held, near_rows):
    del after, after_too
    first = lax.axis_index("e") == 0
    mine, other = joint[4 * HD : (4 + FAR) * HD, :], other_rows[: FAR * HD, :]
    lower = jnp.where(first, mine, other)
    upper = jnp.where(first, other, mine)
    for j in range(4):
        sent[j, : 2 * HD, :] = lower
        sent[j, 2 * HD : 4 * HD, :] = upper
        sent[j, 4 * HD : 6 * HD, :] = joint[2 * HD : 4 * HD, :]
        sent[j, 6 * HD :, :] = prior[...]
    held[...] = joint[: 4 * HD, :]
    near_rows[...] = joint[(4 + FAR) * HD :, :]


def query_rows(gathered, slot, first):
    at = first // 4 * 2 * HD + slot * HD
    return gathered[first % 4 : first % 4 + TILE // HD, at : at + HD, :].reshape(TILE, HD)


def position():
    return lax.axis_index("k"), lax.axis_index("e"), lax.axis_index("x")


def place(distance):
    k, e, x = position()
    return ((lax.rem(k + distance + RING, RING) * 2 + e) * 4 + x) * HD


def sources():
    first = jnp.where(lax.axis_index("c") == 0, -1, 1)
    return [0 * first, first, -first, 2 * first, -2 * first, 3 * first, -3 * first, 4 * first]


def offsets():
    token = lax.broadcasted_iota(jnp.int32, (HD, TILE), 1)
    return lax.rem(token, HD), token - lax.broadcasted_iota(jnp.int32, (HD, TILE), 0)


def tile_of(t):
    per = TILE // HD
    return t // (BLOCKS // per), t % (BLOCKS // per) * per


def masked_scores(spans, order, offset, key_rows, rows, t, cached, start):
    slot, first = tile_of(t)
    begin = CACHE + lax.axis_index("k") * (BLOCKS * HD) + first * HD
    found = dot(key_rows, rows, NT)
    if cached:
        allowed = offset < spans[order[slot]] - begin + start
    else:
        allowed = offset >= start + CACHE - begin
    return jnp.where(allowed, found, MASKED)


def highest(found):
    return jnp.max(found.reshape(HD // 8, 8, found.shape[1]), axis=0)


def near_heads(spans, order, rows, own, gathered, out):
    x = lax.axis_index("x")
    column, _ = offsets()
    behind = column - lax.broadcasted_iota(jnp.int32, (HD, TILE), 0)
    span = jnp.where(
        lax.broadcasted_iota(jnp.int32, (HD, TILE), 1) < HD, spans[order[2]], spans[order[3]]
    )
    found, values = [], []
    for j in range(5):
        if j < 4:
            distance = jnp.where(j < x, x - j, x - j + 4) * HD
            block = jnp.where(j < x, gathered[j, 4 * HD : 6 * HD, :], gathered[j, 6 * HD :, :])
            key_rows, value_rows = block[:HD, :], block[HD:, :]
        else:
            distance = 0
            key_rows, value_rows = own[2 * HD : 3 * HD, :], own[3 * HD :, :]
        far = behind + distance
        found.append(
            jnp.where((far >= 0) & (far < span), dot(key_rows, rows[...], NT), MASKED)
        )
        values.append(value_rows)
    top = highest(found[0])
    for j in range(1, 5):
        top = jnp.maximum(top, highest(found[j]))
    top = jnp.max(top, axis=0, keepdims=True)
    weights = jnp.concatenate(
        [jnp.exp2((f - top) * FACTOR).astype(jnp.bfloat16) for f in found], axis=0
    )
    flipped = jnp.concatenate([v.T for v in values], axis=1)
    flipped = jnp.concatenate([flipped, jnp.ones((STATS, 5 * HD), jnp.bfloat16)], axis=0)
    summed = dot(flipped, weights, NN)
    normal = summed[:HD, :] * (1.0 / summed[HD : HD + 1, :])
    for s in range(2):
        out[s] = normal[:, s * HD : (s + 1) * HD].T.astype(jnp.bfloat16)


def first_kernel(spans, near_rows, queries, *refs):
    kv = refs[: RING - 1]
    sums, tops, near, keys, flipped, scores = refs[RING - 1 :]
    order = head_order(spans)
    distances = sources()
    blocks = []
    for i in range(RING - 1):
        for half in range(2):
            n = len(blocks)
            blocks.append((half == 0, place(distances[i])))
            keys[n * HD : (n + 1) * HD, :] = kv[i][2 * half * HD : (2 * half + 1) * HD, :]
            flipped[0:HD, n * HD : (n + 1) * HD] = kv[i][
                (2 * half + 1) * HD : (2 * half + 2) * HD, :
            ].T
    width = len(blocks) * HD
    flipped[HD:, :] = jnp.ones((STATS, width), jnp.bfloat16)
    _, offset = offsets()

    def score(t):
        slot, first = tile_of(t)
        rows = query_rows(queries, slot, first)
        top = jnp.full((8, TILE), FLOOR, jnp.float32)
        for n, (cached, start) in enumerate(blocks):
            found = masked_scores(
                spans, order, offset, keys[n * HD : (n + 1) * HD, :], rows, t, cached, start
            )
            scores[t % 2, n * HD : (n + 1) * HD, :] = found
            top = jnp.maximum(top, highest(found))
        return jnp.max(top, axis=0, keepdims=True)

    def finish(t, top):
        weights = jnp.concatenate(
            [
                jnp.exp2((scores[t % 2, n * HD : (n + 1) * HD, :] - top) * FACTOR).astype(
                    jnp.bfloat16
                )
                for n in range(len(blocks))
            ],
            axis=0,
        )
        sums[t] = dot(flipped[...], weights, NN)
        tops[t] = jnp.broadcast_to(top, (8, TILE))

    near_heads(spans, order, near_rows, kv[0], queries, near)
    top = score(0)
    for t in range(TILES):
        later = score(t + 1) if t + 1 < TILES else None
        finish(t, top)
        top = later


def write_stats(stats, block, slot, top, total):
    level = jnp.where(total > 0.0, top * FACTOR + jnp.log2(total), MASKED)
    for i in range(3):
        term = level.astype(jnp.bfloat16).astype(jnp.float32)
        stats[block, slot * 4 + i : slot * 4 + i + 1, :] = term
        level = level - term


def second_kernel(spans, queries, last, sums, tops, out, stats):
    order = head_order(spans)
    start = place(sources()[-1])
    _, offset = offsets()
    ones = jnp.ones((STATS, HD), jnp.bfloat16)
    flipped = jnp.concatenate(
        [
            jnp.concatenate([last[HD : 2 * HD, :].T, ones], axis=0),
            jnp.concatenate([last[3 * HD :, :].T, ones], axis=0),
        ],
        axis=1,
    )
    stats[...] = jnp.zeros_like(stats)
    for t in range(TILES):
        slot, first = tile_of(t)
        rows = query_rows(queries, slot, first)
        found = [
            masked_scores(
                spans, order, offset, last[2 * half * HD : (2 * half + 1) * HD, :],
                rows, t, half == 0, start,
            )
            for half in range(2)
        ]
        before = tops[t, 0:1, :]
        top = jnp.max(jnp.maximum(highest(found[0]), highest(found[1])), axis=0, keepdims=True)
        top = jnp.maximum(top, before)
        weights = [jnp.exp2((f - top) * FACTOR).astype(jnp.bfloat16) for f in found]
        summed = sums[t] * jnp.exp2((before - top) * FACTOR) + dot(
            flipped, jnp.concatenate(weights, axis=0), NN
        )
        total = summed[HD : HD + 1, :]
        normal = summed[:HD, :] * (1.0 / jnp.maximum(total, 1e-30))
        for j in range(TILE // HD):
            cut = slice(j * HD, (j + 1) * HD)
            out[first + j, slot * HD : (slot + 1) * HD, :] = normal[:, cut].astype(jnp.bfloat16)
            write_stats(stats, first + j, slot, top[:, cut], total[:, cut])
    out[:, FAR * HD :, :] = stats[...].astype(jnp.bfloat16)


def project_kernel(spans, parts, near, weight, out, kept, attn):
    order = head_order(spans)
    terms = parts[:, FAR * HD :, :].astype(jnp.float32)
    for s in range(FAR):
        level = [
            terms[i, 4 * s : 4 * s + 1] + terms[i, 4 * s + 1 : 4 * s + 2] + terms[i, 4 * s + 2 : 4 * s + 3]
            for i in range(BLOCKS)
        ]
        top = level[0]
        for i in range(1, BLOCKS):
            top = jnp.maximum(top, level[i])
        share = [jnp.exp2(v - top) for v in level]
        total = share[0]
        for i in range(1, BLOCKS):
            total = total + share[i]
        summed = jnp.zeros((HD, HD), jnp.float32)
        for i in range(BLOCKS):
            summed = summed + parts[i, s * HD : (s + 1) * HD, :].astype(jnp.float32) * share[i]
        attn[:, pl.ds(pl.multiple_of(order[s] * HD, HD), HD)] = (
            (summed * (1.0 / total)).T.astype(jnp.bfloat16)
        )
    for s in range(FAR, GROUP):
        attn[:, pl.ds(pl.multiple_of(order[s] * HD, HD), HD)] = near[s - FAR]
    rows = attn[...]
    mine = lax.axis_index("c")
    width = out.shape[2]
    for core, target in ((1 - mine, out), (mine, kept)):
        for f in range(out.shape[0]):
            at = pl.multiple_of((2 * f + core) * width, width)
            product = dot(rows, weight[:, pl.ds(at, width)], NN)
            target[f] = product.astype(target.dtype)


def add_kernel(kept, received, out):
    out[...] = (kept[...] + received[...].astype(jnp.float32)).astype(jnp.bfloat16)


def total_kernel(shares, out):
    total = shares[0].astype(jnp.float32)
    for i in range(1, shares.shape[0]):
        total = total + shares[i].astype(jnp.float32)
    out[...] = total.T.astype(jnp.bfloat16)


def call(kernel, outs, specs, scratch=(), vmem=24, flops=0, moved=0, exps=0):
    single = not isinstance(outs, list)
    return pl.pallas_call(
        kernel,
        out_shape=outs,
        in_specs=specs,
        out_specs=VMEM if single else [VMEM] * len(outs),
        scratch_shapes=list(scratch),
        compiler_params=pltpu.CompilerParams(vmem_limit_bytes=vmem * 2**20),
        cost_estimate=pl.CostEstimate(flops=flops, bytes_accessed=moved, transcendentals=exps),
    )


def per_device(queries, keys, values, cache_keys, cache_values, spans, out_weight):
    bf16, f32 = jnp.bfloat16, jnp.float32
    own, own_rows, handed, joint = call(
        prepare_kernel,
        [
            jax.ShapeDtypeStruct((4 * HD, HD), bf16),
            jax.ShapeDtypeStruct((GROUP * HD, HD), bf16),
            jax.ShapeDtypeStruct((2 * HD, HD), bf16),
            jax.ShapeDtypeStruct((2 * GROUP * HD, HD), bf16),
        ],
        [ANY] * 6,
        [
            pltpu.VMEM((HD, GROUP * HD), bf16),
            pltpu.SMEM((GROUP,), jnp.int32),
            pltpu.SemaphoreType.DMA((6,)),
        ],
        vmem=60,
        moved=2**20,
    )(spans, queries, keys, values, cache_keys, cache_values)
    other_rows = lax.ppermute(own_rows, "e", [(0, 1), (1, 0)])
    prior = lax.ppermute(
        handed, ("k", "e"), [(i, (i + 1) % (2 * RING)) for i in range(2 * RING)]
    )
    routes = [
        [
            (2 * i + c, (i + (1 if c == turn else -1)) % RING * 2 + c)
            for i in range(RING)
            for c in range(2)
        ]
        for turn in range(2)
    ]
    kv, one, two = [own], own, own
    for step in range(RING // 2 - 1):
        one = lax.ppermute(one, ("k", "c"), routes[0])
        two = lax.ppermute(two, ("k", "c"), routes[1])
        kv += [one, two]
        if step == 0:
            one, two, other_rows, prior = lax.optimization_barrier((one, two, other_rows, prior))
    last = lax.ppermute(one, ("k", "c"), routes[0])
    sent, kv[0], near_rows = call(
        spread_kernel,
        [
            jax.ShapeDtypeStruct((4, 8 * HD, HD), bf16),
            jax.ShapeDtypeStruct((4 * HD, HD), bf16),
            jax.ShapeDtypeStruct((2 * HD, HD), bf16),
        ],
        [VMEM] * 3 + [ANY] * 2,
        moved=2**20,
    )(joint, other_rows, prior, kv[1], kv[2])
    grouped = lax.all_to_all(sent, "x", 0, 0, tiled=True)
    near_blocks = 2 * (RING - 1)
    sums, tops, near = call(
        first_kernel,
        [
            jax.ShapeDtypeStruct((TILES, HD + STATS, TILE), f32),
            jax.ShapeDtypeStruct((TILES, 8, TILE), f32),
            jax.ShapeDtypeStruct((2, HD, HD), bf16),
        ],
        [SMEM] + [VMEM] * (RING + 1),
        [
            pltpu.VMEM((near_blocks * HD, HD), bf16),
            pltpu.VMEM((HD + STATS, near_blocks * HD), bf16),
            pltpu.VMEM((2, near_blocks * HD, TILE), f32),
        ],
        flops=4 * 2048 * 1792 * 128,
        moved=4 * 2**20,
        exps=2048 * 1792,
    )(spans, near_rows, grouped, *kv)
    partial = call(
        second_kernel,
        jax.ShapeDtypeStruct((BLOCKS, PIECE, HD), bf16),
        [SMEM] + [VMEM] * 4,
        [pltpu.VMEM((BLOCKS, STATS, HD), f32)],
        flops=4 * 2048 * 256 * 128,
        moved=4 * 2**20,
        exps=2048 * 256,
    )(spans, grouped, last, sums, tops)
    parts = lax.all_to_all(partial, ("e", "x"), 0, 0, tiled=True)
    width = out_weight.shape[1] // 8
    product, kept = call(
        project_kernel,
        [
            jax.ShapeDtypeStruct((4, HD, width), bf16),
            jax.ShapeDtypeStruct((4, HD, width), f32),
        ],
        [SMEM, VMEM, VMEM, VMEM],
        [pltpu.VMEM((HD, GROUP * HD), bf16)],
        flops=2 * 128 * 512 * 4096,
        moved=5 * 2**20,
    )(spans, parts, near, out_weight)
    received = lax.ppermute(product, "c", [(0, 1), (1, 0)])
    halves = call(
        add_kernel,
        jax.ShapeDtypeStruct((4, HD, width), bf16),
        [VMEM] * 2,
        moved=2 * 2**20,
    )(kept, received)
    shares = lax.all_to_all(halves, "y", 0, 0, tiled=True)
    return call(
        total_kernel,
        jax.ShapeDtypeStruct((width, HD), bf16),
        [VMEM],
        moved=2**20,
    )(shares)


def solution(mesh):
    fine = Mesh(mesh.devices.reshape(RING, 2, 4, 4, 2), ("k", "e", "x", "y", "c"))
    seq, head = ("k", "e", "x"), ("y", "c")
    placed = (P(seq, head),) * 5 + (P(head), P(head, None))
    return jax.shard_map(
        per_device, mesh=fine, in_specs=placed, out_specs=P(head, seq), check_vma=False
    )
```
